256 devices in a mesh: ctx: 32 (over z_hi, y, x), tp: 8 (over z_lo, core).
Axes of the slice: x: 4, y: 4, z: 8 (z_hi: 2, z_lo: 4; z = z_hi * 4 + z_lo), core: 2. Of those that a mesh axis runs over, the one named last changes fastest.
Arguments:
- features: bfloat16 [3, 8192, 4096], P(None, 'tp', 'ctx'), may hold values from -6 to 6
- short_filters: bfloat16 [3, 3, 8192], P(None, None, 'tp'), may hold values from -3 to 3
- long_filter: bfloat16 [8192, 4096], P('tp', 'ctx'), may hold values from -0.09375 to 0.09375
- cotangent: bfloat16 [8192, 4096], P('tp', 'ctx'), may hold values from -6 to 6
Outputs:
- feature_grads: float32 [3, 8192, 4096], P(None, 'tp', 'ctx')
- short_grads: float32 [3, 3, 8192], P(None, None, 'tp')
- long_grads: float32 [8192, 4096], P('tp', 'ctx')
The draws below stay inside these ranges and needn't reach their ends.
All inputs are finite; a program needn't handle non-finite values.
Results may differ from the reference program's by a relative error of at most 0.0041.
Values may be sent and summed in bfloat16 or wider, within the bound.
A program may use at most 64 MiB of HBM per device.

```python
import jax
import jax.numpy as jnp
from jax import lax

D = 8192
SHORT = 3
SEQ = 4096


def steps_of(stream_key, shape, cuts, smallest, largest):
    def one(axis_at, shards_of):
        draws = jax.random.uniform(jax.random.fold_in(jax.random.fold_in(stream_key, 6), axis_at), (shards_of,), jnp.float32, smallest / len(cuts), largest / len(cuts))
        return jnp.repeat(jnp.exp(draws), shape[axis_at] // shards_of).reshape((-1,) + (1,) * (len(shape) - axis_at - 1))

    gain = one(*cuts[0])
    for cut in cuts[1:]:
        gain = gain * one(*cut)
    return gain


def noise(rng, dims, scale, bound, cuts=(), dtype=jnp.bfloat16):
    level = steps_of(rng, dims, cuts, -0.22, 0.18) if cuts else 1.0
    entries = jax.random.normal(rng, dims, jnp.float32) * scale * level
    return jnp.minimum(jnp.maximum(entries, -bound), bound).astype(dtype)


def setup_inputs(seed: int = 0) -> dict:
    key_list = jax.random.split(jax.random.key(seed), 5)
    return {
        "features": noise(key_list[0], (3, D, SEQ), 1.0, 6.0, ((1, 8), (2, 32))),
        "short_filters": noise(key_list[1], (3, SHORT, D), 0.5, 3.0, ((2, 8),)),
        "long_filter": noise(key_list[2], (D, SEQ), SEQ ** -0.5, 0.09375, ((0, 8), (1, 32))),
        "cotangent": noise(key_list[3], (D, SEQ), 1.0, 6.0, ((0, 8), (1, 32))),
    }


def short_conv(padded, weights, length):
    width = weights.shape[1]
    total = jnp.zeros(padded.shape[:-1] + (length,), jnp.float32)
    for offset in range(width):
        start = width - 1 - offset
        total = total + weights[:, offset, :, None] * padded[..., start:start + length]
    return total


def group_grads(features, taps, filt, cotan):
    length = features.shape[-1]
    width = taps.shape[1]
    total_len = 2 * length
    signal = features.astype(jnp.float32)
    weights = taps.astype(jnp.float32)
    padded = jnp.pad(signal, ((0, 0), (0, 0), (width - 1, 0)))
    mixed = short_conv(padded, weights, length)
    upstream = cotan.astype(jnp.float32)
    gated = lax.optimization_barrier((mixed[1] * mixed[2]).astype(jnp.bfloat16)).astype(jnp.float32)
    outer = lax.optimization_barrier((upstream * mixed[0]).astype(jnp.bfloat16)).astype(jnp.float32)
    filt_spec = jnp.fft.rfft(filt.astype(jnp.float32), n=total_len)
    gate_spec = jnp.fft.rfft(gated, n=total_len)
    outer_spec = jnp.fft.rfft(outer, n=total_len)
    conv_out = jnp.fft.irfft(filt_spec * gate_spec, n=total_len)[:, :length]
    gate_grad = jnp.fft.irfft(jnp.conj(filt_spec) * outer_spec, n=total_len)[:, :length]
    filt_grad = jnp.fft.irfft(outer_spec * jnp.conj(gate_spec), n=total_len)[:, :length]
    branch_grads = jnp.stack([upstream * conv_out, gate_grad * mixed[2], gate_grad * mixed[1]])
    trailing = jnp.pad(branch_grads, ((0, 0), (0, 0), (0, width - 1)))
    feature_grads = jnp.zeros(branch_grads.shape, jnp.float32)
    for offset in range(width):
        feature_grads = feature_grads + weights[:, offset, :, None] * trailing[..., offset:offset + length]
    short_grads = jnp.stack([jnp.sum(branch_grads * padded[..., width - 1 - offset:width - 1 - offset + length], axis=-1) for offset in range(width)], axis=1)
    return feature_grads, short_grads, filt_grad


def apply_group(items):
    return group_grads(items[0], items[1], items[2], items[3])


def reference(features, short_filters, long_filter, cotangent):
    group_width = min(512, D)
    count = D // group_width
    feat_groups = features.reshape(3, count, group_width, SEQ).transpose(1, 0, 2, 3)
    tap_groups = short_filters.reshape(3, SHORT, count, group_width).transpose(2, 0, 1, 3)
    filt_groups = long_filter.reshape(count, group_width, SEQ)
    cot_groups = cotangent.reshape(count, group_width, SEQ)
    results = lax.map(apply_group, (feat_groups, tap_groups, filt_groups, cot_groups))
    feature_grads = results[0].transpose(1, 0, 2, 3).reshape(3, D, SEQ)
    short_grads = results[1].transpose(1, 2, 0, 3).reshape(3, SHORT, D)
    long_grads = results[2].reshape(D, SEQ)
    return (feature_grads, short_grads, long_grads)
```

```python
import math

import jax
import jax.numpy as jnp
from jax import lax
from jax.sharding import PartitionSpec as P


def from_behind(array, axis, by):
    size = lax.axis_size(axis)
    pairs = [(i, i + by) for i in range(size) if 0 <= i + by < size]
    return lax.ppermute(array, axis, pairs)


def spectral_einsum(form, left, right):
    return jnp.einsum(form, left, right, precision=lax.Precision.HIGH)


def rotation(rows, cols, modulus, sign):
    product = (
        lax.broadcasted_iota(jnp.int32, (rows, cols), 0)
        * lax.broadcasted_iota(jnp.int32, (rows, cols), 1)
        % modulus
    )
    angle = sign * 2.0 * math.pi / modulus * product.astype(jnp.float32)
    return (jnp.cos(angle), jnp.sin(angle))


def spectral_tables(total):
    inner = 128
    outer = total // inner
    return (
        rotation(outer, outer, outer, -1.0),
        rotation(outer, inner, total, -1.0),
        rotation(inner, inner, inner, -1.0),
    )


def forward_spectrum(signal, tables, total):
    first, twiddle, second = tables
    channels, length = signal.shape
    outer = first[0].shape[0]
    padded = jnp.pad(signal, ((0, 0), (0, total - length))).reshape(channels, outer, total // outer)
    real_part = spectral_einsum("kn,cnm->ckm", first[0], padded)
    imag_part = spectral_einsum("kn,cnm->ckm", first[1], padded)
    turned_real = real_part * twiddle[0] - imag_part * twiddle[1]
    turned_imag = real_part * twiddle[1] + imag_part * twiddle[0]
    spec_real = spectral_einsum("ckm,mj->ckj", turned_real, second[0]) - spectral_einsum(
        "ckm,mj->ckj", turned_imag, second[1]
    )
    spec_imag = spectral_einsum("ckm,mj->ckj", turned_real, second[1]) + spectral_einsum(
        "ckm,mj->ckj", turned_imag, second[0]
    )
    return (spec_real, spec_imag)


def inverse_signal(spec_real, spec_imag, tables, total, length):
    first, twiddle, second = tables
    channels = spec_real.shape[0]
    part_real = spectral_einsum("ckj,mj->ckm", spec_real, second[0]) + spectral_einsum(
        "ckj,mj->ckm", spec_imag, second[1]
    )
    part_imag = spectral_einsum("ckj,mj->ckm", spec_imag, second[0]) - spectral_einsum(
        "ckj,mj->ckm", spec_real, second[1]
    )
    turned_real = part_real * twiddle[0] + part_imag * twiddle[1]
    turned_imag = part_imag * twiddle[0] - part_real * twiddle[1]
    signal = spectral_einsum("nk,ckm->cnm", first[0], turned_real) + spectral_einsum(
        "nk,ckm->cnm", first[1], turned_imag
    )
    return signal.reshape(channels, total)[:, :length] / total


def long_core(gated, outer, filt):
    length = gated.shape[1]
    total = 2 * length
    tables = spectral_tables(total)
    filt_real, filt_imag = forward_spectrum(filt, tables, total)
    gate_real, gate_imag = forward_spectrum(gated, tables, total)
    outer_real, outer_imag = forward_spectrum(outer, tables, total)
    conv_out = inverse_signal(
        filt_real * gate_real - filt_imag * gate_imag,
        filt_real * gate_imag + filt_imag * gate_real,
        tables,
        total,
        length,
    )
    gate_grad = inverse_signal(
        filt_real * outer_real + filt_imag * outer_imag,
        filt_real * outer_imag - filt_imag * outer_real,
        tables,
        total,
        length,
    )
    filt_grad = inverse_signal(
        outer_real * gate_real + outer_imag * gate_imag,
        outer_imag * gate_real - outer_real * gate_imag,
        tables,
        total,
        length,
    )
    return (conv_out, gate_grad, filt_grad)


def short_conv(padded, weights, length):
    width = weights.shape[1]
    total = jnp.zeros(padded.shape[:-1] + (length,), jnp.float32)
    for offset in range(width):
        start = width - 1 - offset
        total = total + weights[:, offset, :, None] * padded[..., start : start + length]
    return total


def body(features, short_filters, long_filter, cotangent):
    length_dev = features.shape[-1]
    width = short_filters.shape[1]
    rim = from_behind(features[..., length_dev - (width - 1) :], "ctx", 1)
    signal = features.astype(jnp.float32)
    weights = short_filters.astype(jnp.float32)
    padded = jnp.concatenate([rim.astype(jnp.float32), signal], axis=-1)
    mixed = short_conv(padded, weights, length_dev)
    upstream = cotangent.astype(jnp.float32)
    gated = (mixed[1] * mixed[2]).astype(jnp.bfloat16)
    outer = (upstream * mixed[0]).astype(jnp.bfloat16)
    moved = (
        lax.all_to_all(gated, "ctx", split_axis=0, concat_axis=1, tiled=True),
        lax.all_to_all(outer, "ctx", split_axis=0, concat_axis=1, tiled=True),
        lax.all_to_all(long_filter, "ctx", split_axis=0, concat_axis=1, tiled=True),
    )
    conv_full, grad_full, filt_full = long_core(
        moved[0].astype(jnp.float32), moved[1].astype(jnp.float32), moved[2].astype(jnp.float32)
    )
    conv_full, grad_full, filt_full = (
        array.astype(jnp.bfloat16) for array in (conv_full, grad_full, filt_full)
    )
    back = (
        lax.all_to_all(conv_full, "ctx", split_axis=1, concat_axis=0, tiled=True),
        lax.all_to_all(grad_full, "ctx", split_axis=1, concat_axis=0, tiled=True),
        lax.all_to_all(filt_full, "ctx", split_axis=1, concat_axis=0, tiled=True),
    )
    conv_out, gate_grad, filt_grad = (array.astype(jnp.float32) for array in back)
    branch_grads = jnp.stack([upstream * conv_out, gate_grad * mixed[2], gate_grad * mixed[1]])
    next_rim = from_behind(branch_grads[..., : width - 1], "ctx", -1)
    trailing = jnp.concatenate([branch_grads, next_rim], axis=-1)
    feature_grads = jnp.zeros(branch_grads.shape, jnp.float32)
    for offset in range(width):
        feature_grads = (
            feature_grads
            + weights[:, offset, :, None] * trailing[..., offset : offset + length_dev]
        )
    local_short = jnp.stack(
        [
            jnp.sum(
                branch_grads * padded[..., width - 1 - offset : width - 1 - offset + length_dev],
                axis=-1,
            )
            for offset in range(width)
        ],
        axis=1,
    )
    short_grads = butterfly_sum(local_short, "ctx")
    return (feature_grads, short_grads, filt_grad)


def butterfly_sum(array, axis):
    size = lax.axis_size(axis)
    step = 1
    while step < size:
        array = array + lax.ppermute(array, axis, [(i, i ^ step) for i in range(size)])
        step *= 2
    return array


def solution(mesh):
    return jax.shard_map(
        body,
        mesh=mesh,
        in_specs=(P(None, "tp", "ctx"), P(None, None, "tp"), P("tp", "ctx"), P("tp", "ctx")),
        out_specs=(P(None, "tp", "ctx"), P(None, None, "tp"), P("tp", "ctx")),
        check_vma=False,
    )
```

```python
import functools
import math

import jax
import jax.numpy as jnp
import numpy as np
from jax import lax
from jax.experimental import pallas as pl
from jax.experimental.pallas import tpu as pltpu
from jax.sharding import PartitionSpec as P

MESH = pl.DeviceIdType.MESH
F32, BF16 = jnp.float32, jnp.bfloat16
BLOCKS = 32
PLANE = 16
POS = 128
CH = 1024
OWN = CH // BLOCKS
HALF = OWN // 2
TOTAL = BLOCKS * POS
ROWS = BLOCKS * HALF


def tables():
    k = np.arange(BLOCKS)[:, None] + 0.25
    angle = 2.0 * np.pi * k * np.arange(POS)[None, :] / TOTAL
    turn = np.stack([np.cos(angle), np.sin(angle)], axis=1).astype(np.float32)
    turn = np.broadcast_to(turn[:, :, None, :], (BLOCKS, 2, 8, POS))
    angle = 2.0 * np.pi * np.arange(POS)[:, None] * np.arange(POS)[None, :] / POS
    cos, sin = np.cos(angle), np.sin(angle)
    ahead = np.block([[cos, sin], [-sin, cos]])
    back = np.block([[cos, -sin], [sin, cos]]) / TOTAL

    def split(matrix):
        high = matrix.astype(BF16)
        low = (matrix - high.astype(np.float64)).astype(BF16)
        return np.stack([high, low])

    return np.ascontiguousarray(turn), np.concatenate([split(ahead), split(back)])


def add(a, b):
    return a[0] + b[0], a[1] + b[1]


def sub(a, b):
    return a[0] - b[0], a[1] - b[1]


def quarter(a, sign):
    return (-a[1], a[0]) if sign > 0 else (a[1], -a[0])


def rotate(a, angle):
    c, s = math.cos(angle), math.sin(angle)
    return a[0] * c - a[1] * s, a[0] * s + a[1] * c


def dft4(a, b, c, d, sign):
    e0, e1, o0, o1 = add(a, c), sub(a, c), add(b, d), quarter(sub(b, d), sign)
    return add(e0, o0), add(e1, o1), sub(e0, o0), sub(e1, o1)


def dft8(v, sign):
    even = dft4(v[0], v[2], v[4], v[6], sign)
    odd = dft4(v[1], v[3], v[5], v[7], sign)
    r = math.sqrt(0.5)
    a, b = odd[1], odd[3]
    if sign > 0:
        t1 = ((a[0] - a[1]) * r, (a[0] + a[1]) * r)
        t3 = ((b[0] + b[1]) * -r, (b[0] - b[1]) * r)
    else:
        t1 = ((a[0] + a[1]) * r, (a[1] - a[0]) * r)
        t3 = ((b[1] - b[0]) * r, (b[0] + b[1]) * -r)
    turned = (odd[0], t1, quarter(odd[2], sign), t3)
    return [add(e, t) for e, t in zip(even, turned)] + [sub(e, t) for e, t in zip(even, turned)]


def blocks_ahead(load, stage, turn_ref, store):
    c, s, r = math.cos(math.pi / 8), math.sin(math.pi / 8), math.sqrt(0.5)
    for b0 in range(8):
        x0, x1, x2, x3 = (load(b0 + 8 * b1) for b1 in range(4))
        x2 = x2 * r
        e0, e1 = (x0 + x2, x2), (x0 - x2, -x2)
        u1, u3 = (x1 * c, x1 * s), (x3 * s, x3 * c)
        o0, o1 = add(u1, u3), quarter(sub(u1, u3), 1)
        for k1, value in enumerate((add(e0, o0), add(e1, o1), sub(e0, o0), sub(e1, o1))):
            if b0:
                value = rotate(value, 2.0 * math.pi * (k1 + 0.25) * b0 / 32)
            stage[k1, b0, 0], stage[k1, b0, 1] = value
    for k1 in range(4):
        spectrum = dft8([(stage[k1, b0, 0], stage[k1, b0, 1]) for b0 in range(8)], 1)
        for k0, (re, im) in enumerate(spectrum):
            k = k1 + 4 * k0
            cos, sin = turn_ref[k, 0], turn_ref[k, 1]
            store(k, re * cos - im * sin, re * sin + im * cos)


def blocks_back(load, stage, turn_ref, store):
    for k1 in range(4):
        terms = []
        for k0 in range(8):
            k = k1 + 4 * k0
            re, im = load(k)
            cos, sin = turn_ref[k, 0], turn_ref[k, 1]
            terms.append((re * cos + im * sin, im * cos - re * sin))
        for b0, value in enumerate(dft8(terms, -1)):
            if b0:
                value = rotate(value, -2.0 * math.pi * (k1 + 0.25) * b0 / 32)
            stage[k1, b0, 0], stage[k1, b0, 1] = value
    for b0 in range(8):
        terms = [(stage[k1, b0, 0], stage[k1, b0, 1]) for k1 in range(4)]
        for b1, (re, im) in enumerate(dft4(*terms, -1)):
            angle = math.pi * b1 / 8
            store(b0 + 8 * b1, re * math.cos(angle) + im * math.sin(angle) if b1 else re)


def product(values, weights):
    high = values.astype(BF16)
    low = (values - high.astype(F32)).astype(BF16)
    dot = functools.partial(jnp.dot, preferred_element_type=F32)
    return dot(high, weights[0]) + dot(low, weights[0]) + dot(high, weights[1])


def kernel(
    feat, taps, filt, cot, turn, waves,
    fgrad, sgrad, lgrad,
    taps_t, wide, behind, mixed, halo_out, halo_in,
    go_out, filt_in, go_in, times, freqs, spec, stage, conv_out, long_out, conv_in, long_in,
    sums, sums_t, part_out, part_in, whole_in, rim_in,
    send, recv,
):
    me = lax.axis_index("ctx")
    low = lax.rem(me, PLANE)
    plane = me - low

    def to(device):
        return {"ctx": device}

    def each(count, step):
        lax.fori_loop(0, count, lambda i, c: (step(i), c)[1], 0)

    def remote(src, dst, sem, device):
        return pltpu.make_async_remote_copy(
            src_ref=src, dst_ref=dst, send_sem=send.at[sem], recv_sem=recv.at[sem],
            device_id=to(device), device_id_type=MESH,
        )

    def await_all(ref, sem, way):
        pltpu.make_async_copy(ref, ref, way.at[sem]).wait()

    barrier = pltpu.get_barrier_semaphore()
    each(
        BLOCKS - 1,
        lambda i: pl.semaphore_signal(
            barrier, inc=1, device_id=to(lax.rem(me + i + 1, BLOCKS)), device_id_type=MESH
        ),
    )

    row = lax.broadcasted_iota(jnp.int32, (16, POS), 0)
    lane = lax.broadcasted_iota(jnp.int32, (16, POS), 1)
    rim = jnp.zeros((16, CH), F32)
    for b in range(3):
        pick = (lane == row + (126 - 2 * b)) & (row >= 2 * b) & (row < 2 * b + 2)
        rim = rim + lax.dot_general(
            pick.astype(BF16), feat[b], (((1,), (1,)), ((), ())), preferred_element_type=F32
        )
    halo_out[...] = rim.astype(BF16)
    taps_t[...] = jnp.zeros_like(taps_t)
    for b in range(3):
        taps_t[3 * b : 3 * b + 3, :] = taps[b].astype(F32)
    turned = taps_t[...].T.astype(BF16)
    from_row = lax.broadcasted_iota(jnp.int32, (POS, POS), 0)
    for r in range(9):
        wide[r] = jnp.dot(turned, (from_row == r).astype(BF16), preferred_element_type=F32)

    pl.semaphore_wait(barrier, BLOCKS - 1)

    @pl.when(me < BLOCKS - 1)
    def _():
        remote(halo_out, halo_in, 0, me + 1).start()

    def send_filter(i):
        p = lax.rem(me + i + 1, BLOCKS)
        remote(filt.at[pl.ds(pl.multiple_of(p * OWN, OWN), OWN)], filt_in.at[me], 1, p).start()

    each(BLOCKS - 1, send_filter)
    filt_in[me] = filt[pl.ds(pl.multiple_of(me * OWN, OWN), OWN), :]

    @pl.when(me > 0)
    def _():
        remote(halo_out, halo_in, 0, me).wait_recv()

    taps_t[...] = jnp.zeros_like(taps_t)

    @pl.when(me > 0)
    def _():
        taps_t[0:16, :] = halo_in[...].astype(F32)

    turned = taps_t[...].T.astype(BF16)
    to_lane = lax.broadcasted_iota(jnp.int32, (POS, POS), 1)
    for b in range(3):
        pick = (to_lane == from_row + (126 - 2 * b)) & (from_row >= 2 * b) & (from_row < 2 * b + 2)
        behind[b] = jnp.dot(turned, pick.astype(BF16), preferred_element_type=F32)

    def make_go(r0, target):
        rows = pl.ds(r0, 16)
        m = []
        for b in range(3):
            x, past = feat[b, rows, :].astype(F32), behind[b, rows, :]
            x1 = pltpu.roll(jnp.where(lane >= 127, past, x), 1, 1)
            x2 = pltpu.roll(jnp.where(lane >= 126, past, x), 2, 1)
            m.append(wide[3 * b, rows, :] * x + wide[3 * b + 1, rows, :] * x1 + wide[3 * b + 2, rows, :] * x2)
        mixed[0, rows, :], mixed[1, rows, :] = m[1], m[2]
        target[0] = (m[1] * m[2]).astype(BF16)
        target[1] = (cot[rows, :].astype(F32) * m[0]).astype(BF16)

    for h in range(2):

        def send_go(i, h=h):
            p = lax.rem(me + i + 1, BLOCKS)
            make_go(pl.multiple_of(p * OWN + HALF * h, 16), go_out.at[h, p])
            remote(go_out.at[h, p], go_in.at[h, me], 2 + h, p).start()

        each(BLOCKS - 1, send_go)
        make_go(pl.multiple_of(me * OWN + HALF * h, 16), go_in.at[h, me])

    def transform(h):
        def spread(b):
            times[0, b] = filt_in[b, HALF * h : HALF * h + HALF, :].astype(F32)
            times[1, b] = go_in[h, b, 0].astype(F32)
            times[2, b] = go_in[h, b, 1].astype(F32)

        each(BLOCKS, spread)

        def ahead(i):
            s, q = i // 2, pl.multiple_of(lax.rem(i, 2) * 8, 8)

            def store(k, re, im):
                freqs[s, pl.ds(k * HALF + q, 8), 0:POS] = re
                freqs[s, pl.ds(k * HALF + q, 8), POS : 2 * POS] = im

            blocks_ahead(lambda b: times[s, b, pl.ds(q, 8), :], stage, turn, store)

        each(6, ahead)

        def positions(i):
            rows = pl.ds(pl.multiple_of(i * 256, 256), 256)
            for s in range(3):
                spec[s] = product(freqs[s, rows, :], waves.at[0:2])
            f, g, o = ((spec[s, :, 0:POS], spec[s, :, POS : 2 * POS]) for s in range(3))
            pairs = (
                (f[0] * g[0] - f[1] * g[1], f[0] * g[1] + f[1] * g[0]),
                (f[0] * o[0] + f[1] * o[1], f[0] * o[1] - f[1] * o[0]),
                (g[0] * o[0] + g[1] * o[1], g[0] * o[1] - g[1] * o[0]),
            )
            for s, (re, im) in enumerate(pairs):
                spec[s + 3, :, 0:POS], spec[s + 3, :, POS : 2 * POS] = re, im
            for s in range(3):
                freqs[s, rows, :] = product(spec[s + 3], waves.at[2:4])

        each(ROWS // 256, positions)

        def back(i):
            s, q = i // 2, pl.multiple_of(lax.rem(i, 2) * 8, 8)

            def load(k):
                rows = pl.ds(k * HALF + q, 8)
                return freqs[s, rows, 0:POS], freqs[s, rows, POS : 2 * POS]

            def store(b, value):
                times[s, b, pl.ds(q, 8), :] = value

            blocks_back(load, stage, turn, store)

        each(6, back)

        def pack(b):
            conv_out[h, b, 0] = times[0, b].astype(BF16)
            conv_out[h, b, 1] = times[1, b].astype(BF16)
            long_out[h, b] = times[2, b].astype(BF16)

        each(BLOCKS, pack)

    def send_conv(h):
        def step(i):
            p = lax.rem(me + i + 1, BLOCKS)
            remote(conv_out.at[h, p], conv_in.at[h, me], 4 + h, p).start()

        each(BLOCKS - 1, step)
        conv_in[h, me] = conv_out[h, me]

    await_all(filt_in.at[0 : BLOCKS - 1], 1, recv)
    await_all(go_in.at[0, 0 : BLOCKS - 1], 2, recv)
    transform(0)
    send_conv(0)
    await_all(go_in.at[1, 0 : BLOCKS - 1], 3, recv)
    transform(1)
    send_conv(1)
    for h in range(2):

        def send_long(i, h=h):
            p = lax.rem(me + i + 1, BLOCKS)
            remote(long_out.at[h, p], long_in.at[h, me], 6 + h, p).start()

        each(BLOCKS - 1, send_long)
        long_in[h, me] = long_out[h, me]

    def finish(h, e):
        rows = pl.ds(pl.multiple_of(e * OWN + HALF * h, 16), 16)
        conv, grad = conv_in[h, e, 0].astype(F32), conv_in[h, e, 1].astype(F32)
        branch = (cot[rows, :].astype(F32) * conv, grad * mixed[1, rows, :], grad * mixed[0, rows, :])
        out = jnp.zeros((16, POS), F32)
        for b, g in enumerate(branch):
            x, past = feat[b, rows, :].astype(F32), behind[b, rows, :]
            g1, g2 = pltpu.roll(g, 127, 1), pltpu.roll(g, 126, 1)
            fgrad[b, rows, :] = (
                wide[3 * b, rows, :] * g
                + wide[3 * b + 1, rows, :] * jnp.where(lane < 127, g1, 0.0)
                + wide[3 * b + 2, rows, :] * jnp.where(lane < 126, g2, 0.0)
            )
            dots = (g * x, g1 * jnp.where(lane >= 127, past, x), g2 * jnp.where(lane >= 126, past, x))
            for j, dot in enumerate(dots):
                out = jnp.where(lane == 3 * b + j, jnp.sum(dot, axis=1, keepdims=True), out)
            first = 16 + 2 * b
            out = jnp.where((lane >= first) & (lane < first + 2), pltpu.roll(g, first, 1), out)
        sums[rows, :] = out

    for h in range(2):
        await_all(conv_in.at[h, 0 : BLOCKS - 1], 4 + h, recv)
        each(BLOCKS, functools.partial(finish, h))

    sums_t[...] = sums[...].T

    @pl.when(me > 0)
    def _():
        remote(sums_t.at[16:24], rim_in, 8, me - 1).start()

    for q in range(PLANE):
        r, c = q // 8, q % 8
        part_out[q] = sums_t[8 * r : 8 * r + 8, POS * c : POS * c + POS]

    def send_part(i):
        q = lax.rem(low + i + 1, PLANE)
        remote(part_out.at[q], part_in.at[low], 9, plane + q).start()

    each(PLANE - 1, send_part)
    part_in[low] = part_out[low]

    for h in range(2):
        await_all(long_in.at[h, 0 : BLOCKS - 1], 6 + h, recv)

        def unpack(e, h=h):
            rows = pl.ds(pl.multiple_of(e * OWN + HALF * h, 16), 16)
            lgrad[rows, :] = long_in[h, e].astype(F32)

        each(BLOCKS, unpack)

    await_all(part_in.at[0 : PLANE - 1], 9, recv)
    total = part_in[0]
    for q in range(1, PLANE):
        total = total + part_in[q]
    whole_in[me] = total

    def send_whole(i):
        p = lax.rem(me + i + 1, BLOCKS)
        remote(whole_in.at[me], whole_in.at[me], 10, p).start()

    each(BLOCKS - 1, send_whole)

    taps_t[...] = jnp.zeros_like(taps_t)

    @pl.when(me < BLOCKS - 1)
    def _():
        remote(rim_in, rim_in, 8, me).wait_recv()
        taps_t[0:8, :] = rim_in[...]

    sums[...] = taps_t[...].T

    def add_rim(e):
        rows = pl.ds(pl.multiple_of(e * 16, 16), 16)
        ahead = sums[rows, :]
        for b in range(3):
            g1 = jnp.where(lane >= 127, pltpu.roll(ahead, 127 - 2 * b, 1), 0.0)
            g2 = jnp.where(lane >= 126, pltpu.roll(ahead, 126 - 2 * b, 1), 0.0)
            fgrad[b, rows, :] += wide[3 * b + 1, rows, :] * g1 + wide[3 * b + 2, rows, :] * g2

    each(CH // 16, add_rim)

    await_all(whole_in.at[0 : BLOCKS - 1], 10, recv)
    for q in range(8):
        lanes = pl.ds(POS * q, POS)
        top = whole_in[q] + whole_in[PLANE + q]
        rest = whole_in[8 + q] + whole_in[PLANE + 8 + q]
        sgrad[0, :, lanes], sgrad[1, :, lanes] = top[0:3], top[3:6]
        sgrad[2, 0:2, lanes], sgrad[2, 2:3, lanes] = top[6:8], rest[0:1]

    @pl.when(me < BLOCKS - 1)
    def _():
        remote(halo_out, halo_in, 0, me).wait_send()

    @pl.when(me > 0)
    def _():
        remote(sums_t.at[16:24], rim_in, 8, me).wait_send()

    await_all(filt_in.at[0 : BLOCKS - 1], 1, send)
    for h in range(2):
        await_all(go_out.at[h, 0 : BLOCKS - 1], 2 + h, send)
        await_all(conv_out.at[h, 0 : BLOCKS - 1], 4 + h, send)
        await_all(long_out.at[h, 0 : BLOCKS - 1], 6 + h, send)
    await_all(part_out.at[0 : PLANE - 1], 9, send)
    await_all(whole_in.at[0 : BLOCKS - 1], 10, send)


def body(features, short_filters, long_filter, cotangent):
    turn, waves = tables()
    vmem = pl.BlockSpec(memory_space=pltpu.VMEM)
    return pl.pallas_call(
        kernel,
        out_shape=(
            jax.ShapeDtypeStruct((3, CH, POS), F32),
            jax.ShapeDtypeStruct((3, 3, CH), F32),
            jax.ShapeDtypeStruct((CH, POS), F32),
        ),
        in_specs=[vmem] * 6,
        out_specs=(vmem,) * 3,
        scratch_shapes=[
            pltpu.VMEM((POS, CH), F32),
            pltpu.VMEM((9, CH, POS), F32),
            pltpu.VMEM((3, CH, POS), F32),
            pltpu.VMEM((2, CH, POS), F32),
            pltpu.VMEM((16, CH), BF16),
            pltpu.VMEM((16, CH), BF16),
            pltpu.VMEM((2, BLOCKS, 2, HALF, POS), BF16),
            pltpu.VMEM((BLOCKS, OWN, POS), BF16),
            pltpu.VMEM((2, BLOCKS, 2, HALF, POS), BF16),
            pltpu.VMEM((3, BLOCKS, HALF, POS), F32),
            pltpu.VMEM((3, ROWS, 2 * POS), F32),
            pltpu.VMEM((6, 256, 2 * POS), F32),
            pltpu.VMEM((4, 8, 2, 8, POS), F32),
            pltpu.VMEM((2, BLOCKS, 2, HALF, POS), BF16),
            pltpu.VMEM((2, BLOCKS, HALF, POS), BF16),
            pltpu.VMEM((2, BLOCKS, 2, HALF, POS), BF16),
            pltpu.VMEM((2, BLOCKS, HALF, POS), BF16),
            pltpu.VMEM((CH, POS), F32),
            pltpu.VMEM((POS, CH), F32),
            pltpu.VMEM((PLANE, 8, POS), F32),
            pltpu.VMEM((PLANE, 8, POS), F32),
            pltpu.VMEM((BLOCKS, 8, POS), F32),
            pltpu.VMEM((8, CH), F32),
            pltpu.SemaphoreType.DMA((11,)),
            pltpu.SemaphoreType.DMA((11,)),
        ],
        compiler_params=pltpu.CompilerParams(
            collective_id=0, has_side_effects=True, vmem_limit_bytes=48 * 2**20
        ),
    )(features, short_filters, long_filter, cotangent, jnp.asarray(turn), jnp.asarray(waves))


def solution(mesh):
    return jax.shard_map(
        body,
        mesh=mesh,
        in_specs=(P(None, "tp", "ctx"), P(None, None, "tp"), P("tp", "ctx"), P("tp", "ctx")),
        out_specs=(P(None, "tp", "ctx"), P(None, None, "tp"), P("tp", "ctx")),
        check_vma=False,
    )
```

```python
import functools
import math

import jax
import jax.numpy as jnp
import numpy as np
from jax import lax
from jax.experimental import pallas as pl
from jax.experimental.pallas import tpu as pltpu
from jax.sharding import PartitionSpec as P

MESH = pl.DeviceIdType.MESH
F32, BF16 = jnp.float32, jnp.bfloat16
BLOCKS = 32
PLANE = 16
POS = 128
CH = 1024
OWN = CH // BLOCKS
HALF = OWN // 2
TOTAL = BLOCKS * POS
ROWS = BLOCKS * HALF


def tables():
    k = np.arange(BLOCKS)[:, None] + 0.25
    angle = 2.0 * np.pi * k * np.arange(POS)[None, :] / TOTAL
    turn = np.stack([np.cos(angle), np.sin(angle)], axis=1).astype(np.float32)
    turn = np.broadcast_to(turn[:, :, None, :], (BLOCKS, 2, 8, POS))
    angle = 2.0 * np.pi * np.arange(POS)[:, None] * np.arange(POS)[None, :] / POS
    cos, sin = np.cos(angle), np.sin(angle)
    ahead = np.block([[cos, sin], [-sin, cos]])
    back = np.block([[cos, -sin], [sin, cos]]) / TOTAL

    def split(matrix):
        high = matrix.astype(BF16)
        low = (matrix - high.astype(np.float64)).astype(BF16)
        return np.stack([high, low])

    return np.ascontiguousarray(turn), np.concatenate([split(ahead), split(back)])


def movers():
    shift = np.zeros((4, 2 * POS, 2 * POS), np.float32)
    for n in range(POS):
        if n >= 1:
            shift[:3, n - 1, n] = 1
        if n >= 2:
            shift[:3, n - 2, POS + n] = 1
        for part in (0, POS):
            if n + 1 < POS:
                shift[3, part + n + 1, n] = 1
            if n + 2 < POS:
                shift[3, part + n + 2, POS + n] = 1
    spots = np.zeros((15 * POS, POS), np.float32)
    edge = np.zeros((2 * POS, 3 * POS), np.float32)
    for r in range(9):
        spots[r * POS : r * POS + POS, r] = 1
    for b in range(3):
        shift[b, POS + 2 * b + 1, 0] = 1
        shift[b, POS + 2 * b, POS] = 1
        shift[b, POS + 2 * b + 1, POS + 1] = 1
        for part in range(2):
            for t in range(2):
                spots[(9 + 2 * b + part) * POS + t, 16 + 2 * b + t] = 1
                edge[part * POS + 2 * b + t, POS * b + 126 + t] = 1
    return shift.astype(BF16), spots.astype(BF16), edge.astype(BF16)


def add(a, b):
    return a[0] + b[0], a[1] + b[1]


def sub(a, b):
    return a[0] - b[0], a[1] - b[1]


def quarter(a, sign):
    return (-a[1], a[0]) if sign > 0 else (a[1], -a[0])


def rotate(a, angle):
    c, s = math.cos(angle), math.sin(angle)
    return a[0] * c - a[1] * s, a[0] * s + a[1] * c


def dft4(a, b, c, d, sign):
    e0, e1, o0, o1 = add(a, c), sub(a, c), add(b, d), quarter(sub(b, d), sign)
    return add(e0, o0), add(e1, o1), sub(e0, o0), sub(e1, o1)


def dft8(v, sign):
    even = dft4(v[0], v[2], v[4], v[6], sign)
    odd = dft4(v[1], v[3], v[5], v[7], sign)
    r = math.sqrt(0.5)
    a, b = odd[1], odd[3]
    if sign > 0:
        t1 = ((a[0] - a[1]) * r, (a[0] + a[1]) * r)
        t3 = ((b[0] + b[1]) * -r, (b[0] - b[1]) * r)
    else:
        t1 = ((a[0] + a[1]) * r, (a[1] - a[0]) * r)
        t3 = ((b[1] - b[0]) * r, (b[0] + b[1]) * -r)
    turned = (odd[0], t1, quarter(odd[2], sign), t3)
    return [add(e, t) for e, t in zip(even, turned)] + [sub(e, t) for e, t in zip(even, turned)]


def blocks_ahead(load, stage, turn_ref, store):
    c, s, r = math.cos(math.pi / 8), math.sin(math.pi / 8), math.sqrt(0.5)
    for b0 in range(8):
        x0, x1, x2, x3 = (load(b0 + 8 * b1) for b1 in range(4))
        x2 = x2 * r
        e0, e1 = (x0 + x2, x2), (x0 - x2, -x2)
        u1, u3 = (x1 * c, x1 * s), (x3 * s, x3 * c)
        o0, o1 = add(u1, u3), quarter(sub(u1, u3), 1)
        for k1, value in enumerate((add(e0, o0), add(e1, o1), sub(e0, o0), sub(e1, o1))):
            if b0:
                value = rotate(value, 2.0 * math.pi * (k1 + 0.25) * b0 / 32)
            stage[k1, b0, 0], stage[k1, b0, 1] = value
    for k1 in range(4):
        spectrum = dft8([(stage[k1, b0, 0], stage[k1, b0, 1]) for b0 in range(8)], 1)
        for k0, (re, im) in enumerate(spectrum):
            k = k1 + 4 * k0
            cos, sin = turn_ref[k, 0], turn_ref[k, 1]
            store(k, re * cos - im * sin, re * sin + im * cos)


def blocks_back(load, stage, turn_ref, store):
    for k1 in range(4):
        terms = []
        for k0 in range(8):
            k = k1 + 4 * k0
            re, im = load(k)
            cos, sin = turn_ref[k, 0], turn_ref[k, 1]
            terms.append((re * cos + im * sin, im * cos - re * sin))
        for b0, value in enumerate(dft8(terms, -1)):
            if b0:
                value = rotate(value, -2.0 * math.pi * (k1 + 0.25) * b0 / 32)
            stage[k1, b0, 0], stage[k1, b0, 1] = value
    for b0 in range(8):
        terms = [(stage[k1, b0, 0], stage[k1, b0, 1]) for k1 in range(4)]
        for b1, (re, im) in enumerate(dft4(*terms, -1)):
            angle = math.pi * b1 / 8
            store(b0 + 8 * b1, re * math.cos(angle) + im * math.sin(angle) if b1 else re)


def halves(values):
    high = values.astype(BF16)
    return high, (values - high.astype(F32)).astype(BF16)


def product(values, weights):
    high, low = halves(values)
    dot = functools.partial(jnp.dot, preferred_element_type=F32)
    return dot(high, weights[0]) + dot(low, weights[0]) + dot(high, weights[1])


def kernel(
    feat_hbm, taps_hbm, filt_hbm, cot_hbm, turn_hbm, waves_hbm, shift_hbm, spots_hbm, edge_hbm,
    fgrad_hbm, sgrad_hbm, lgrad_hbm,
    fgrad, sgrad, lgrad, feat, taps, filt, cot, turn, waves, shift, spots, edge,
    taps_t, rim_t, wide, shifted, mixed, pieces, dots, moved, halo_out, halo_in,
    go_out, filt_in, go_in, times, freqs, spec, stage, conv_out, long_out, conv_in, long_in,
    sums, sums_t, part_out, part_in, whole_in, rim_in,
    send, recv, conv_recv, local,
):
    me = lax.axis_index("ctx")
    low = lax.rem(me, PLANE)
    plane = me - low

    def to(device):
        return {"ctx": device}

    def each(count, step, unroll=1):
        lax.fori_loop(0, count, lambda i, c: (step(i), c)[1], 0, unroll=unroll)

    def remote(src, dst, sem, device):
        return pltpu.make_async_remote_copy(
            src_ref=src, dst_ref=dst, send_sem=send.at[sem], recv_sem=recv.at[sem],
            device_id=to(device), device_id_type=MESH,
        )

    def await_all(ref, sem, way):
        pltpu.make_async_copy(ref, ref, way.at[sem]).wait()

    def across(i):
        return PLANE - plane + lax.rem(low + i, PLANE)

    def within(i):
        return plane + lax.rem(low + i + 1, PLANE)

    def to_all(step):
        each(PLANE, lambda i: step(across(i)))
        each(PLANE - 1, lambda i: step(within(i)))

    loads = [
        pltpu.make_async_copy(src, dst, local.at[i])
        for i, (src, dst) in enumerate(
            (
                (feat_hbm, feat), (filt_hbm, filt), (taps_hbm, taps), (shift_hbm, shift), (cot_hbm, cot),
                (turn_hbm, turn), (waves_hbm, waves), (spots_hbm, spots), (edge_hbm, edge),
            )
        )
    ]
    for load in loads:
        load.start()
    barrier = pltpu.get_barrier_semaphore()
    to_all(lambda p: pl.semaphore_signal(barrier, inc=1, device_id=to(p), device_id_type=MESH))

    row = lax.broadcasted_iota(jnp.int32, (16, POS), 0)
    lane = lax.broadcasted_iota(jnp.int32, (16, POS), 1)
    rim = jnp.zeros((16, CH), F32)
    loads[0].wait()
    for b in range(3):
        pick = (lane == row + (126 - 2 * b)) & (row >= 2 * b) & (row < 2 * b + 2)
        rim = rim + lax.dot_general(
            pick.astype(BF16), feat[b], (((1,), (1,)), ((), ())), preferred_element_type=F32
        )
    halo_out[...] = rim.astype(BF16)
    loads[1].wait()
    pl.semaphore_wait(barrier, BLOCKS - 1)

    @pl.when(me < BLOCKS - 1)
    def _():
        remote(halo_out, halo_in, 0, me + 1).start()

    def send_filter(p):
        remote(filt.at[pl.ds(pl.multiple_of(p * OWN, OWN), OWN)], filt_in.at[me], 1, p).start()

    to_all(send_filter)
    filt_in[me] = filt[pl.ds(pl.multiple_of(me * OWN, OWN), OWN), :]

    for load in loads[2:]:
        load.wait()
    taps_t[...] = jnp.zeros_like(taps_t)
    for b in range(3):
        taps_t[3 * b : 3 * b + 3, :] = taps[b].astype(F32)
    turned = taps_t[...].T.astype(BF16)
    from_row = lax.broadcasted_iota(jnp.int32, (POS, POS), 0)
    for r in range(9):
        wide[r] = jnp.dot(turned, (from_row == r).astype(BF16), preferred_element_type=F32)


    rim_t[...] = jnp.zeros_like(rim_t)

    @pl.when(me > 0)
    def _():
        remote(halo_out, halo_in, 0, me).wait_recv()
        rim_t[0:16, :] = halo_in[...].astype(F32)

    behind = rim_t[...].T.astype(BF16)
    for b in range(3):
        shifted[b] = jnp.dot(
            jnp.concatenate([feat[b], behind], axis=1), shift[b], preferred_element_type=F32
        ).astype(BF16)

    def make_go(r0, target):
        rows = pl.ds(r0, 16)
        m = []
        for b in range(3):
            x = feat[b, rows, :].astype(F32)
            x1, x2 = shifted[b, rows, 0:POS].astype(F32), shifted[b, rows, POS : 2 * POS].astype(F32)
            m.append(wide[3 * b, rows, :] * x + wide[3 * b + 1, rows, :] * x1 + wide[3 * b + 2, rows, :] * x2)
        mixed[0, rows, :], mixed[1, rows, :] = m[1], m[2]
        target[0] = (m[1] * m[2]).astype(BF16)
        target[1] = (cot[rows, :].astype(F32) * m[0]).astype(BF16)

    for h in range(2):

        def send_go(p, h=h):
            make_go(pl.multiple_of(p * OWN + HALF * h, 16), go_out.at[h, p])
            remote(go_out.at[h, p], go_in.at[h, me], 2 + h, p).start()

        to_all(send_go)
        make_go(pl.multiple_of(me * OWN + HALF * h, 16), go_in.at[h, me])

    def transform(h):
        def spread(b):
            times[0, b] = filt_in[b, HALF * h : HALF * h + HALF, :].astype(F32)
            times[1, b] = go_in[h, b, 0].astype(F32)
            times[2, b] = go_in[h, b, 1].astype(F32)

        each(BLOCKS, spread, 4)

        def ahead(i):
            s, q = i // 2, pl.multiple_of(lax.rem(i, 2) * 8, 8)

            def store(k, re, im):
                freqs[s, pl.ds(k * HALF + q, 8), 0:POS] = re
                freqs[s, pl.ds(k * HALF + q, 8), POS : 2 * POS] = im

            blocks_ahead(lambda b: times[s, b, pl.ds(q, 8), :], stage, turn, store)

        each(6, ahead)

        for s in range(3):
            spec[s] = product(freqs[s], waves.at[0:2])

        def pairs(i):
            rows = pl.ds(pl.multiple_of(i * 8, 8), 8)
            f, g, o = ((spec[s, rows, 0:POS], spec[s, rows, POS : 2 * POS]) for s in range(3))
            both = (
                (f[0] * g[0] - f[1] * g[1], f[0] * g[1] + f[1] * g[0]),
                (f[0] * o[0] + f[1] * o[1], f[0] * o[1] - f[1] * o[0]),
                (g[0] * o[0] + g[1] * o[1], g[0] * o[1] - g[1] * o[0]),
            )
            for s, (re, im) in enumerate(both):
                freqs[s, rows, 0:POS], freqs[s, rows, POS : 2 * POS] = re, im

        each(ROWS // 8, pairs, 4)
        for s in range(3):
            spec[s] = product(freqs[s], waves.at[2:4])

        def back(i):
            s, q = i // 2, pl.multiple_of(lax.rem(i, 2) * 8, 8)

            def load(k):
                rows = pl.ds(k * HALF + q, 8)
                return spec[s, rows, 0:POS], spec[s, rows, POS : 2 * POS]

            def store(b, value):
                times[s, b, pl.ds(q, 8), :] = value

            blocks_back(load, stage, turn, store)

        each(6, back)

        def pack(b):
            conv_out[h, b, 0] = times[0, b].astype(BF16)
            conv_out[h, b, 1] = times[1, b].astype(BF16)
            long_out[h, b] = times[2, b].astype(BF16)

        each(BLOCKS, pack, 4)

    def send_conv(h):
        def step(p):
            pltpu.make_async_remote_copy(
                src_ref=conv_out.at[h, p], dst_ref=conv_in.at[h, me], send_sem=send.at[4 + h],
                recv_sem=conv_recv.at[h, me], device_id=to(p), device_id_type=MESH,
            ).start()

        to_all(step)
        conv_in[h, me] = conv_out[h, me]

    await_all(filt_in.at[0 : BLOCKS - 1], 1, recv)
    await_all(go_in.at[0, 0 : BLOCKS - 1], 2, recv)
    transform(0)
    send_conv(0)
    await_all(go_in.at[1, 0 : BLOCKS - 1], 3, recv)
    transform(1)
    send_conv(1)
    for h in range(2):

        def send_long(p, h=h):
            remote(long_out.at[h, p], long_in.at[h, me], 6 + h, p).start()

        to_all(send_long)
        long_in[h, me] = long_out[h, me]

    def finish(h, e):
        rows = pl.ds(pl.multiple_of(e * OWN + HALF * h, 16), 16)
        here = pl.ds(pl.multiple_of(e * HALF, 16), 16)
        conv, grad = conv_in[h, e, 0].astype(F32), conv_in[h, e, 1].astype(F32)
        branch = (cot[rows, :].astype(F32) * conv, grad * mixed[1, rows, :], grad * mixed[0, rows, :])
        for b, g in enumerate(branch):
            pieces[h, b, here, 0:POS], pieces[h, b, here, POS : 2 * POS] = halves(g)
            past = (
                feat[b, rows, :], shifted[b, rows, 0:POS], shifted[b, rows, POS : 2 * POS]
            )
            for j, x in enumerate(past):
                k = (3 * b + j) * POS
                dots[here, k : k + POS] = (g * x.astype(F32)).astype(BF16)

    def add_up(h):
        dot = functools.partial(jnp.dot, preferred_element_type=F32)
        total = dot(dots[...], spots[0 : 9 * POS, :])
        for b in range(3):
            k = (9 + 2 * b) * POS
            total = total + dot(pieces[h, b], spots[k : k + 2 * POS, :])
        sums[:, h] = total.reshape(BLOCKS, HALF, POS)

    def trail(h):
        for b in range(3):
            moved[b] = jnp.dot(pieces[h, b], shift[3], preferred_element_type=F32)

        def step(e):
            rows = pl.ds(pl.multiple_of(e * OWN + HALF * h, 16), 16)
            here = pl.ds(pl.multiple_of(e * HALF, 16), 16)
            for b in range(3):
                g = pieces[h, b, here, 0:POS].astype(F32) + pieces[h, b, here, POS : 2 * POS].astype(F32)
                fgrad[b, rows, :] = (
                    wide[3 * b, rows, :] * g
                    + wide[3 * b + 1, rows, :] * moved[b, here, 0:POS]
                    + wide[3 * b + 2, rows, :] * moved[b, here, POS : 2 * POS]
                )

        each(BLOCKS, step, 2)

    for h in range(2):
        finish(h, me)

        def arrived(e, h=h):
            pltpu.make_async_copy(conv_in.at[h, e], conv_in.at[h, e], conv_recv.at[h, e]).wait()
            finish(h, e)

        each(PLANE - 1, lambda i: arrived(plane + lax.rem(low + PLANE - 1 - i, PLANE)))
        each(PLANE, lambda i: arrived(PLANE - plane + lax.rem(low + PLANE - i, PLANE)))
        add_up(h)
        if h == 0:
            trail(h)

    sums_t[...] = sums[...].reshape(CH, POS).T

    @pl.when(me > 0)
    def _():
        remote(sums_t.at[16:24], rim_in, 8, me - 1).start()

    for q in range(PLANE):
        r, c = q // 8, q % 8
        part_out[q] = sums_t[8 * r : 8 * r + 8, POS * c : POS * c + POS]

    def send_part(i):
        q = lax.rem(low + i + 1, PLANE)
        remote(part_out.at[q], part_in.at[low], 9, plane + q).start()

    each(PLANE - 1, send_part)
    part_in[low] = part_out[low]

    trail(1)
    await_all(part_in.at[0 : PLANE - 1], 9, recv)
    total = part_in[0]
    for q in range(1, PLANE):
        total = total + part_in[q]
    whole_in[me] = total

    to_all(lambda p: remote(whole_in.at[me], whole_in.at[me], 10, p).start())

    for h in range(2):
        await_all(long_in.at[h, 0 : BLOCKS - 1], 6 + h, recv)

        def unpack(e, h=h):
            rows = pl.ds(pl.multiple_of(e * OWN + HALF * h, 16), 16)
            lgrad[rows, :] = long_in[h, e].astype(F32)

        each(BLOCKS, unpack)

    stores = [
        pltpu.make_async_copy(src, dst, local.at[i])
        for i, (src, dst) in enumerate(((fgrad, fgrad_hbm), (sgrad, sgrad_hbm), (lgrad, lgrad_hbm)))
    ]
    stores[2].start()

    rim_t[...] = jnp.zeros_like(rim_t)

    @pl.when(me < BLOCKS - 1)
    def _():
        remote(rim_in, rim_in, 8, me).wait_recv()
        for b in range(3):
            first, second = rim_in[2 * b : 2 * b + 1, :], rim_in[2 * b + 1 : 2 * b + 2, :]
            w1, w2 = taps_t[3 * b + 1 : 3 * b + 2, :], taps_t[3 * b + 2 : 3 * b + 3, :]
            rim_t[2 * b : 2 * b + 1, :] = w2 * first
            rim_t[2 * b + 1 : 2 * b + 2, :] = w1 * first + w2 * second

    beyond = jnp.dot(
        jnp.concatenate(halves(rim_t[...].T), axis=1), edge[...], preferred_element_type=F32
    )
    for b in range(3):
        fgrad[b] += beyond[:, POS * b : POS * b + POS]
    stores[0].start()

    await_all(whole_in.at[0 : BLOCKS - 1], 10, recv)
    for q in range(8):
        lanes = pl.ds(POS * q, POS)
        top = whole_in[q] + whole_in[PLANE + q]
        rest = whole_in[8 + q] + whole_in[PLANE + 8 + q]
        sgrad[0, :, lanes], sgrad[1, :, lanes] = top[0:3], top[3:6]
        sgrad[2, 0:2, lanes], sgrad[2, 2:3, lanes] = top[6:8], rest[0:1]

    stores[1].start()

    @pl.when(me < BLOCKS - 1)
    def _():
        remote(halo_out, halo_in, 0, me).wait_send()

    @pl.when(me > 0)
    def _():
        remote(sums_t.at[16:24], rim_in, 8, me).wait_send()

    await_all(filt_in.at[0 : BLOCKS - 1], 1, send)
    for h in range(2):
        await_all(go_out.at[h, 0 : BLOCKS - 1], 2 + h, send)
        await_all(conv_out.at[h, 0 : BLOCKS - 1], 4 + h, send)
        await_all(long_out.at[h, 0 : BLOCKS - 1], 6 + h, send)
    await_all(part_out.at[0 : PLANE - 1], 9, send)
    await_all(whole_in.at[0 : BLOCKS - 1], 10, send)
    for store in stores:
        store.wait()


def body(features, short_filters, long_filter, cotangent):
    turn, waves = tables()
    shift, spots, edge = movers()
    hbm = pl.BlockSpec(memory_space=pl.ANY)
    return pl.pallas_call(
        kernel,
        out_shape=(
            jax.ShapeDtypeStruct((3, CH, POS), F32),
            jax.ShapeDtypeStruct((3, 3, CH), F32),
            jax.ShapeDtypeStruct((CH, POS), F32),
        ),
        in_specs=[hbm] * 9,
        out_specs=(hbm,) * 3,
        scratch_shapes=[
            pltpu.VMEM((3, CH, POS), F32),
            pltpu.VMEM((3, 3, CH), F32),
            pltpu.VMEM((CH, POS), F32),
            pltpu.VMEM((3, CH, POS), BF16),
            pltpu.VMEM((3, 3, CH), BF16),
            pltpu.VMEM((CH, POS), BF16),
            pltpu.VMEM((CH, POS), BF16),
            pltpu.VMEM((BLOCKS, 2, 8, POS), F32),
            pltpu.VMEM((4, 2 * POS, 2 * POS), BF16),
            pltpu.VMEM((4, 2 * POS, 2 * POS), BF16),
            pltpu.VMEM((15 * POS, POS), BF16),
            pltpu.VMEM((2 * POS, 3 * POS), BF16),
            pltpu.VMEM((POS, CH), F32),
            pltpu.VMEM((POS, CH), F32),
            pltpu.VMEM((9, CH, POS), F32),
            pltpu.VMEM((3, CH, 2 * POS), BF16),
            pltpu.VMEM((2, CH, POS), F32),
            pltpu.VMEM((2, 3, ROWS, 2 * POS), BF16),
            pltpu.VMEM((ROWS, 9 * POS), BF16),
            pltpu.VMEM((3, ROWS, 2 * POS), F32),
            pltpu.VMEM((16, CH), BF16),
            pltpu.VMEM((16, CH), BF16),
            pltpu.VMEM((2, BLOCKS, 2, HALF, POS), BF16),
            pltpu.VMEM((BLOCKS, OWN, POS), BF16),
            pltpu.VMEM((2, BLOCKS, 2, HALF, POS), BF16),
            pltpu.VMEM((3, BLOCKS, HALF, POS), F32),
            pltpu.VMEM((3, ROWS, 2 * POS), F32),
            pltpu.VMEM((3, ROWS, 2 * POS), F32),
            pltpu.VMEM((4, 8, 2, 8, POS), F32),
            pltpu.VMEM((2, BLOCKS, 2, HALF, POS), BF16),
            pltpu.VMEM((2, BLOCKS, HALF, POS), BF16),
            pltpu.VMEM((2, BLOCKS, 2, HALF, POS), BF16),
            pltpu.VMEM((2, BLOCKS, HALF, POS), BF16),
            pltpu.VMEM((BLOCKS, 2, HALF, POS), F32),
            pltpu.VMEM((POS, CH), F32),
            pltpu.VMEM((PLANE, 8, POS), F32),
            pltpu.VMEM((PLANE, 8, POS), F32),
            pltpu.VMEM((BLOCKS, 8, POS), F32),
            pltpu.VMEM((8, CH), F32),
            pltpu.SemaphoreType.DMA((11,)),
            pltpu.SemaphoreType.DMA((11,)),
            pltpu.SemaphoreType.DMA((2, BLOCKS)),
            pltpu.SemaphoreType.DMA((9,)),
        ],
        compiler_params=pltpu.CompilerParams(
            collective_id=0, has_side_effects=True, vmem_limit_bytes=60 * 2**20
        ),
    )(features, short_filters, long_filter, cotangent, *map(jnp.asarray, (turn, waves, shift, spots, edge)))


def solution(mesh):
    return jax.shard_map(
        body,
        mesh=mesh,
        in_specs=(P(None, "tp", "ctx"), P(None, None, "tp"), P("tp", "ctx"), P("tp", "ctx")),
        out_specs=(P(None, "tp", "ctx"), P(None, None, "tp"), P("tp", "ctx")),
        check_vma=False,
    )
```

```python
import functools
import math

import jax
import jax.numpy as jnp
import numpy as np
from jax import lax
from jax.experimental import pallas as pl
from jax.experimental.pallas import tpu as pltpu
from jax.sharding import PartitionSpec as P

MESH = pl.DeviceIdType.MESH
F32, BF16 = jnp.float32, jnp.bfloat16
BLOCKS = 32
PLANE = 16
POS = 128
CH = 1024
OWN = CH // BLOCKS
HALF = OWN // 2
TOTAL = BLOCKS * POS
ROWS = BLOCKS * HALF


def tables():
    k = np.arange(BLOCKS)[:, None] + 0.25
    angle = 2.0 * np.pi * k * np.arange(POS)[None, :] / TOTAL
    turn = np.stack([np.cos(angle), np.sin(angle)], axis=1).astype(np.float32)
    turn = np.broadcast_to(turn[:, :, None, :], (BLOCKS, 2, 8, POS))
    angle = 2.0 * np.pi * np.arange(POS)[:, None] * np.arange(POS)[None, :] / POS
    cos, sin = np.cos(angle), np.sin(angle)
    ahead = np.block([[cos, sin], [-sin, cos]])
    back = np.block([[cos, -sin], [sin, cos]]) / TOTAL

    def split(matrix):
        high = matrix.astype(BF16)
        low = (matrix - high.astype(np.float64)).astype(BF16)
        return np.stack([high, low])

    return np.ascontiguousarray(turn), np.concatenate([split(ahead), split(back)])


def movers():
    shift = np.zeros((4, 2 * POS, 2 * POS), np.float32)
    for n in range(POS):
        if n >= 1:
            shift[:3, n - 1, n] = 1
        if n >= 2:
            shift[:3, n - 2, POS + n] = 1
        for part in (0, POS):
            if n + 1 < POS:
                shift[3, part + n + 1, n] = 1
            if n + 2 < POS:
                shift[3, part + n + 2, POS + n] = 1
    spots = np.zeros((15 * POS, POS), np.float32)
    edge = np.zeros((2 * POS, 3 * POS), np.float32)
    for r in range(9):
        spots[r * POS : r * POS + POS, r] = 1
    for b in range(3):
        shift[b, POS + 2 * b + 1, 0] = 1
        shift[b, POS + 2 * b, POS] = 1
        shift[b, POS + 2 * b + 1, POS + 1] = 1
        for part in range(2):
            for t in range(2):
                spots[(9 + 2 * b + part) * POS + t, 16 + 2 * b + t] = 1
                edge[part * POS + 2 * b + t, POS * b + 126 + t] = 1
    return shift.astype(BF16), spots.astype(BF16), edge.astype(BF16)


def add(a, b):
    return a[0] + b[0], a[1] + b[1]


def sub(a, b):
    return a[0] - b[0], a[1] - b[1]


def quarter(a, sign):
    return (-a[1], a[0]) if sign > 0 else (a[1], -a[0])


def rotate(a, angle):
    c, s = math.cos(angle), math.sin(angle)
    return a[0] * c - a[1] * s, a[0] * s + a[1] * c


def dft4(a, b, c, d, sign):
    e0, e1, o0, o1 = add(a, c), sub(a, c), add(b, d), quarter(sub(b, d), sign)
    return add(e0, o0), add(e1, o1), sub(e0, o0), sub(e1, o1)


def dft8(v, sign):
    even = dft4(v[0], v[2], v[4], v[6], sign)
    odd = dft4(v[1], v[3], v[5], v[7], sign)
    r = math.sqrt(0.5)
    a, b = odd[1], odd[3]
    if sign > 0:
        t1 = ((a[0] - a[1]) * r, (a[0] + a[1]) * r)
        t3 = ((b[0] + b[1]) * -r, (b[0] - b[1]) * r)
    else:
        t1 = ((a[0] + a[1]) * r, (a[1] - a[0]) * r)
        t3 = ((b[1] - b[0]) * r, (b[0] + b[1]) * -r)
    turned = (odd[0], t1, quarter(odd[2], sign), t3)
    return [add(e, t) for e, t in zip(even, turned)] + [sub(e, t) for e, t in zip(even, turned)]


def blocks_ahead(load, stage, turn_ref, store):
    c, s, r = math.cos(math.pi / 8), math.sin(math.pi / 8), math.sqrt(0.5)
    for b0 in range(8):
        x0, x1, x2, x3 = (load(b0 + 8 * b1) for b1 in range(4))
        x2 = x2 * r
        e0, e1 = (x0 + x2, x2), (x0 - x2, -x2)
        u1, u3 = (x1 * c, x1 * s), (x3 * s, x3 * c)
        o0, o1 = add(u1, u3), quarter(sub(u1, u3), 1)
        for k1, value in enumerate((add(e0, o0), add(e1, o1), sub(e0, o0), sub(e1, o1))):
            if b0:
                value = rotate(value, 2.0 * math.pi * (k1 + 0.25) * b0 / 32)
            stage[k1, b0, 0], stage[k1, b0, 1] = value
    for k1 in range(4):
        spectrum = dft8([(stage[k1, b0, 0], stage[k1, b0, 1]) for b0 in range(8)], 1)
        for k0, (re, im) in enumerate(spectrum):
            k = k1 + 4 * k0
            cos, sin = turn_ref[k, 0], turn_ref[k, 1]
            store(k, re * cos - im * sin, re * sin + im * cos)


def blocks_back(load, stage, turn_ref, store):
    for k1 in range(4):
        terms = []
        for k0 in range(8):
            k = k1 + 4 * k0
            re, im = load(k)
            cos, sin = turn_ref[k, 0], turn_ref[k, 1]
            terms.append((re * cos + im * sin, im * cos - re * sin))
        for b0, value in enumerate(dft8(terms, -1)):
            if b0:
                value = rotate(value, -2.0 * math.pi * (k1 + 0.25) * b0 / 32)
            stage[k1, b0, 0], stage[k1, b0, 1] = value
    for b0 in range(8):
        terms = [(stage[k1, b0, 0], stage[k1, b0, 1]) for k1 in range(4)]
        for b1, (re, im) in enumerate(dft4(*terms, -1)):
            angle = math.pi * b1 / 8
            store(b0 + 8 * b1, re * math.cos(angle) + im * math.sin(angle) if b1 else re)


def halves(values):
    high = values.astype(BF16)
    return high, (values - high.astype(F32)).astype(BF16)


def product(values, weights):
    high, low = halves(values)
    dot = functools.partial(jnp.dot, preferred_element_type=F32)
    return dot(high, weights[0]) + dot(low, weights[0]) + dot(high, weights[1])


def kernel(
    feat_hbm, taps_hbm, filt_hbm, cot_hbm, turn_hbm, waves_hbm, shift_hbm, spots_hbm, edge_hbm,
    fgrad_hbm, sgrad_hbm, lgrad_hbm,
    fgrad, sgrad, lgrad, feat, taps, filt, cot, turn, waves, shift, spots, edge,
    taps_t, rim_t, wide, shifted, mixed, pieces, dots, moved, halo_out, halo_in,
    go_out, filt_in, go_in, times, freqs, spec, paired, stage, conv_out, long_out, conv_in, long_in,
    sums, sums_t, part_out, part_in, whole_in, rim_in,
    send, recv, conv_recv, local,
):
    me = lax.axis_index("ctx")
    low = lax.rem(me, PLANE)
    plane = me - low

    def to(device):
        return {"ctx": device}

    def each(count, step, unroll=1):
        lax.fori_loop(0, count, lambda i, c: (step(i), c)[1], 0, unroll=unroll)

    def remote(src, dst, sem, device):
        return pltpu.make_async_remote_copy(
            src_ref=src, dst_ref=dst, send_sem=send.at[sem], recv_sem=recv.at[sem],
            device_id=to(device), device_id_type=MESH,
        )

    def await_all(ref, sem, way):
        pltpu.make_async_copy(ref, ref, way.at[sem]).wait()

    def across(i):
        return PLANE - plane + lax.rem(low + i, PLANE)

    def within(i):
        return plane + lax.rem(low + i + 1, PLANE)

    def to_all(step):
        each(PLANE, lambda i: step(across(i)))
        each(PLANE - 1, lambda i: step(within(i)))

    loads = [
        pltpu.make_async_copy(src, dst, local.at[i])
        for i, (src, dst) in enumerate(
            (
                (feat_hbm, feat), (filt_hbm, filt), (taps_hbm, taps), (shift_hbm, shift), (cot_hbm, cot),
                (turn_hbm, turn), (waves_hbm, waves), (spots_hbm, spots), (edge_hbm, edge),
            )
        )
    ]
    barrier = pltpu.get_barrier_semaphore()
    to_all(lambda p: pl.semaphore_signal(barrier, inc=1, device_id=to(p), device_id_type=MESH))
    for load in loads:
        load.start()

    row = lax.broadcasted_iota(jnp.int32, (16, POS), 0)
    lane = lax.broadcasted_iota(jnp.int32, (16, POS), 1)
    rim = jnp.zeros((16, CH), F32)
    loads[0].wait()
    for b in range(3):
        pick = (lane == row + (126 - 2 * b)) & (row >= 2 * b) & (row < 2 * b + 2)
        rim = rim + lax.dot_general(
            pick.astype(BF16), feat[b], (((1,), (1,)), ((), ())), preferred_element_type=F32
        )
    halo_out[...] = rim.astype(BF16)
    loads[1].wait()
    pl.semaphore_wait(barrier, BLOCKS - 1)

    @pl.when(me < BLOCKS - 1)
    def _():
        remote(halo_out, halo_in, 0, me + 1).start()

    def send_filter(p):
        remote(filt.at[pl.ds(pl.multiple_of(p * OWN, OWN), OWN)], filt_in.at[me], 1, p).start()

    to_all(send_filter)
    filt_in[me] = filt[pl.ds(pl.multiple_of(me * OWN, OWN), OWN), :]

    for load in loads[2:]:
        load.wait()
    taps_t[...] = jnp.zeros_like(taps_t)
    for b in range(3):
        taps_t[3 * b : 3 * b + 3, :] = taps[b].astype(F32)
    turned = taps_t[...].T.astype(BF16)
    from_row = lax.broadcasted_iota(jnp.int32, (POS, POS), 0)
    for r in range(9):
        wide[r] = jnp.dot(turned, (from_row == r).astype(BF16), preferred_element_type=F32)


    rim_t[...] = jnp.zeros_like(rim_t)

    @pl.when(me > 0)
    def _():
        remote(halo_out, halo_in, 0, me).wait_recv()
        rim_t[0:16, :] = halo_in[...].astype(F32)

    behind = rim_t[...].T.astype(BF16)
    for b in range(3):
        shifted[b] = jnp.dot(
            jnp.concatenate([feat[b], behind], axis=1), shift[b], preferred_element_type=F32
        ).astype(BF16)

    def make_go(r0, target):
        rows = pl.ds(r0, 16)
        m = []
        for b in range(3):
            x = feat[b, rows, :].astype(F32)
            x1, x2 = shifted[b, rows, 0:POS].astype(F32), shifted[b, rows, POS : 2 * POS].astype(F32)
            m.append(wide[3 * b, rows, :] * x + wide[3 * b + 1, rows, :] * x1 + wide[3 * b + 2, rows, :] * x2)
        mixed[0, rows, :], mixed[1, rows, :] = m[1], m[2]
        target[0] = (m[1] * m[2]).astype(BF16)
        target[1] = (cot[rows, :].astype(F32) * m[0]).astype(BF16)

    for h in range(2):

        def send_go(p, h=h):
            make_go(pl.multiple_of(p * OWN + HALF * h, 16), go_out.at[h, p])
            remote(go_out.at[h, p], go_in.at[h, me], 2 + h, p).start()

        to_all(send_go)
        make_go(pl.multiple_of(me * OWN + HALF * h, 16), go_in.at[h, me])

    def transform(h):
        def spread(b):
            times[0, b] = filt_in[b, HALF * h : HALF * h + HALF, :].astype(F32)
            times[1, b] = go_in[h, b, 0].astype(F32)
            times[2, b] = go_in[h, b, 1].astype(F32)

        each(BLOCKS, spread, 4)

        def ahead(i):
            s, q = i // 2, pl.multiple_of(lax.rem(i, 2) * 8, 8)

            def store(k, re, im):
                freqs[s, pl.ds(k * HALF + q, 8), 0:POS] = re
                freqs[s, pl.ds(k * HALF + q, 8), POS : 2 * POS] = im

            blocks_ahead(lambda b: times[s, b, pl.ds(q, 8), :], stage, turn, store)

        each(6, ahead)

        for s in range(3):
            spec[s] = product(freqs[s], waves.at[0:2])

        def pairs(i):
            rows = pl.ds(pl.multiple_of(i * 16, 16), 16)
            f, g, o = ((spec[s, rows, 0:POS], spec[s, rows, POS : 2 * POS]) for s in range(3))
            both = (
                (f[0] * g[0] - f[1] * g[1], f[0] * g[1] + f[1] * g[0]),
                (f[0] * o[0] + f[1] * o[1], f[0] * o[1] - f[1] * o[0]),
                (g[0] * o[0] + g[1] * o[1], g[0] * o[1] - g[1] * o[0]),
            )
            for s, (re, im) in enumerate(both):
                paired[s, rows, 0:POS] = re.astype(BF16)
                paired[s, rows, POS : 2 * POS] = im.astype(BF16)

        each(ROWS // 16, pairs, 2)
        for s in range(3):
            spec[s] = jnp.dot(paired[s], waves[2], preferred_element_type=F32) + jnp.dot(
                paired[s], waves[3], preferred_element_type=F32
            )

        def back(i):
            s, q = i // 2, pl.multiple_of(lax.rem(i, 2) * 8, 8)

            def load(k):
                rows = pl.ds(k * HALF + q, 8)
                return spec[s, rows, 0:POS], spec[s, rows, POS : 2 * POS]

            def store(b, value):
                times[s, b, pl.ds(q, 8), :] = value

            blocks_back(load, stage, turn, store)

        each(6, back)

        def pack(b):
            conv_out[h, b, 0] = times[0, b].astype(BF16)
            conv_out[h, b, 1] = times[1, b].astype(BF16)
            long_out[h, b] = times[2, b].astype(BF16)

        each(BLOCKS, pack, 4)

    def send_conv(h):
        def step(p):
            pltpu.make_async_remote_copy(
                src_ref=conv_out.at[h, p], dst_ref=conv_in.at[h, me], send_sem=send.at[4 + h],
                recv_sem=conv_recv.at[h, me], device_id=to(p), device_id_type=MESH,
            ).start()

        to_all(step)
        conv_in[h, me] = conv_out[h, me]

    await_all(filt_in.at[0 : BLOCKS - 1], 1, recv)
    await_all(go_in.at[0, 0 : BLOCKS - 1], 2, recv)
    transform(0)
    send_conv(0)
    await_all(go_in.at[1, 0 : BLOCKS - 1], 3, recv)
    transform(1)
    send_conv(1)
    def finish(h, e):
        rows = pl.ds(pl.multiple_of(e * OWN + HALF * h, 16), 16)
        here = pl.ds(pl.multiple_of(e * HALF, 16), 16)
        conv, grad = conv_in[h, e, 0].astype(F32), conv_in[h, e, 1].astype(F32)
        branch = (cot[rows, :].astype(F32) * conv, grad * mixed[1, rows, :], grad * mixed[0, rows, :])
        for b, g in enumerate(branch):
            pieces[h, b, here, 0:POS], pieces[h, b, here, POS : 2 * POS] = halves(g)
            past = (
                feat[b, rows, :], shifted[b, rows, 0:POS], shifted[b, rows, POS : 2 * POS]
            )
            for j, x in enumerate(past):
                k = (3 * b + j) * POS
                dots[here, k : k + POS] = (g * x.astype(F32)).astype(BF16)

    def add_up(h):
        dot = functools.partial(jnp.dot, preferred_element_type=F32)
        total = dot(dots[...], spots[0 : 9 * POS, :])
        for b in range(3):
            k = (9 + 2 * b) * POS
            total = total + dot(pieces[h, b], spots[k : k + 2 * POS, :])
        sums[:, h] = total.reshape(BLOCKS, HALF, POS)

    def trail(h):
        for b in range(3):
            moved[b] = jnp.dot(pieces[h, b], shift[3], preferred_element_type=F32)

        def step(e):
            rows = pl.ds(pl.multiple_of(e * OWN + HALF * h, 16), 16)
            here = pl.ds(pl.multiple_of(e * HALF, 16), 16)
            for b in range(3):
                g = pieces[h, b, here, 0:POS].astype(F32) + pieces[h, b, here, POS : 2 * POS].astype(F32)
                fgrad[b, rows, :] = (
                    wide[3 * b, rows, :] * g
                    + wide[3 * b + 1, rows, :] * moved[b, here, 0:POS]
                    + wide[3 * b + 2, rows, :] * moved[b, here, POS : 2 * POS]
                )

        each(BLOCKS, step, 2)

    for h in range(2):
        finish(h, me)

        def arrived(e, h=h):
            pltpu.make_async_copy(conv_in.at[h, e], conv_in.at[h, e], conv_recv.at[h, e]).wait()
            finish(h, e)

        each(PLANE - 1, lambda i: arrived(plane + lax.rem(low + PLANE - 1 - i, PLANE)))
        each(PLANE, lambda i: arrived(PLANE - plane + lax.rem(low + PLANE - i, PLANE)))
        add_up(h)
        if h == 0:
            trail(h)

        if h == 0:
            await_all(conv_out.at[1, 0 : BLOCKS - 1], 5, send)
            for k in range(2):

                def send_long(p, k=k):
                    remote(long_out.at[k, p], long_in.at[k, me], 6 + k, p).start()

                to_all(send_long)
                long_in[k, me] = long_out[k, me]


    sums_t[...] = sums[...].reshape(CH, POS).T

    @pl.when(me > 0)
    def _():
        remote(sums_t.at[16:24], rim_in, 8, me - 1).start()

    for r in range(9):
        for c in range(8):
            q, k = (8 * r + c) // 5, (8 * r + c) % 5
            part_out[q, k : k + 1] = sums_t[r : r + 1, POS * c : POS * c + POS]

    part_out[14, 2:5] = jnp.zeros((3, POS), F32)
    part_out[15] = jnp.zeros((5, POS), F32)

    def send_part(i):
        q = lax.rem(low + i + 1, PLANE)
        remote(part_out.at[q], part_in.at[low], 9, plane + q).start()

    each(PLANE - 1, send_part)
    part_in[low] = part_out[low]

    trail(1)
    await_all(part_in.at[0 : PLANE - 1], 9, recv)
    total = part_in[0]
    for q in range(1, PLANE):
        total = total + part_in[q]
    whole_in[me] = total

    to_all(lambda p: remote(whole_in.at[me], whole_in.at[me], 10, p).start())

    stores = [
        pltpu.make_async_copy(src, dst, local.at[i])
        for i, (src, dst) in enumerate(((fgrad, fgrad_hbm), (sgrad, sgrad_hbm), (lgrad, lgrad_hbm)))
    ]
    rim_t[...] = jnp.zeros_like(rim_t)

    @pl.when(me < BLOCKS - 1)
    def _():
        remote(rim_in, rim_in, 8, me).wait_recv()
        for b in range(3):
            first, second = rim_in[2 * b : 2 * b + 1, :], rim_in[2 * b + 1 : 2 * b + 2, :]
            w1, w2 = taps_t[3 * b + 1 : 3 * b + 2, :], taps_t[3 * b + 2 : 3 * b + 3, :]
            rim_t[2 * b : 2 * b + 1, :] = w2 * first
            rim_t[2 * b + 1 : 2 * b + 2, :] = w1 * first + w2 * second

    beyond = jnp.dot(
        jnp.concatenate(halves(rim_t[...].T), axis=1), edge[...], preferred_element_type=F32
    )
    for b in range(3):
        fgrad[b] += beyond[:, POS * b : POS * b + POS]
    stores[0].start()

    for h in range(2):
        await_all(long_in.at[h, 0 : BLOCKS - 1], 6 + h, recv)

        def unpack(e, h=h):
            rows = pl.ds(pl.multiple_of(e * OWN + HALF * h, 16), 16)
            lgrad[rows, :] = long_in[h, e].astype(F32)

        each(BLOCKS, unpack)

    stores[2].start()

    await_all(whole_in.at[0 : BLOCKS - 1], 10, recv)
    for r in range(9):
        for c in range(8):
            q, k = (8 * r + c) // 5, (8 * r + c) % 5
            sgrad[r // 3, r % 3 : r % 3 + 1, POS * c : POS * c + POS] = (
                whole_in[q, k : k + 1] + whole_in[PLANE + q, k : k + 1]
            )
    stores[1].start()

    @pl.when(me < BLOCKS - 1)
    def _():
        remote(halo_out, halo_in, 0, me).wait_send()

    @pl.when(me > 0)
    def _():
        remote(sums_t.at[16:24], rim_in, 8, me).wait_send()

    await_all(filt_in.at[0 : BLOCKS - 1], 1, send)
    for h in range(2):
        await_all(go_out.at[h, 0 : BLOCKS - 1], 2 + h, send)
        if h == 0:
            await_all(conv_out.at[h, 0 : BLOCKS - 1], 4 + h, send)
        await_all(long_out.at[h, 0 : BLOCKS - 1], 6 + h, send)
    await_all(part_out.at[0 : PLANE - 1], 9, send)
    await_all(whole_in.at[0 : BLOCKS - 1], 10, send)
    for store in stores:
        store.wait()


def relay_kernel(fgrad, sgrad, lgrad, fgrad_out, sgrad_out, lgrad_out, fgrad_v, sgrad_v, lgrad_v, sems):
    parts = [(fgrad.at[b], fgrad_v.at[b], fgrad_out.at[b]) for b in range(3)]
    parts += [(lgrad, lgrad_v, lgrad_out), (sgrad, sgrad_v, sgrad_out)]
    loads = [pltpu.make_async_copy(a, b, sems.at[0, i]) for i, (a, b, _) in enumerate(parts)]
    stores = [pltpu.make_async_copy(b, c, sems.at[1, i]) for i, (_, b, c) in enumerate(parts)]
    for load in loads:
        load.start()
    for load, store in zip(loads, stores):
        load.wait()
        store.start()
    for store in stores:
        store.wait()


def body(features, short_filters, long_filter, cotangent):
    turn, waves = tables()
    shift, spots, edge = movers()
    hbm = pl.BlockSpec(memory_space=pl.ANY)
    shapes = (
        jax.ShapeDtypeStruct((3, CH, POS), F32),
        jax.ShapeDtypeStruct((3, 3, CH), F32),
        jax.ShapeDtypeStruct((CH, POS), F32),
    )
    results = pl.pallas_call(
        kernel,
        out_shape=shapes,
        in_specs=[hbm] * 9,
        out_specs=(hbm,) * 3,
        scratch_shapes=[
            pltpu.VMEM((3, CH, POS), F32),
            pltpu.VMEM((3, 3, CH), F32),
            pltpu.VMEM((CH, POS), F32),
            pltpu.VMEM((3, CH, POS), BF16),
            pltpu.VMEM((3, 3, CH), BF16),
            pltpu.VMEM((CH, POS), BF16),
            pltpu.VMEM((CH, POS), BF16),
            pltpu.VMEM((BLOCKS, 2, 8, POS), F32),
            pltpu.VMEM((4, 2 * POS, 2 * POS), BF16),
            pltpu.VMEM((4, 2 * POS, 2 * POS), BF16),
            pltpu.VMEM((15 * POS, POS), BF16),
            pltpu.VMEM((2 * POS, 3 * POS), BF16),
            pltpu.VMEM((POS, CH), F32),
            pltpu.VMEM((POS, CH), F32),
            pltpu.VMEM((9, CH, POS), F32),
            pltpu.VMEM((3, CH, 2 * POS), BF16),
            pltpu.VMEM((2, CH, POS), F32),
            pltpu.VMEM((2, 3, ROWS, 2 * POS), BF16),
            pltpu.VMEM((ROWS, 9 * POS), BF16),
            pltpu.VMEM((3, ROWS, 2 * POS), F32),
            pltpu.VMEM((16, CH), BF16),
            pltpu.VMEM((16, CH), BF16),
            pltpu.VMEM((2, BLOCKS, 2, HALF, POS), BF16),
            pltpu.VMEM((BLOCKS, OWN, POS), BF16),
            pltpu.VMEM((2, BLOCKS, 2, HALF, POS), BF16),
            pltpu.VMEM((3, BLOCKS, HALF, POS), F32),
            pltpu.VMEM((3, ROWS, 2 * POS), F32),
            pltpu.VMEM((3, ROWS, 2 * POS), F32),
            pltpu.VMEM((3, ROWS, 2 * POS), BF16),
            pltpu.VMEM((4, 8, 2, 8, POS), F32),
            pltpu.VMEM((2, BLOCKS, 2, HALF, POS), BF16),
            pltpu.VMEM((2, BLOCKS, HALF, POS), BF16),
            pltpu.VMEM((2, BLOCKS, 2, HALF, POS), BF16),
            pltpu.VMEM((2, BLOCKS, HALF, POS), BF16),
            pltpu.VMEM((BLOCKS, 2, HALF, POS), F32),
            pltpu.VMEM((POS, CH), F32),
            pltpu.VMEM((PLANE, 5, POS), F32),
            pltpu.VMEM((PLANE, 5, POS), F32),
            pltpu.VMEM((BLOCKS, 5, POS), F32),
            pltpu.VMEM((8, CH), F32),
            pltpu.SemaphoreType.DMA((11,)),
            pltpu.SemaphoreType.DMA((11,)),
            pltpu.SemaphoreType.DMA((2, BLOCKS)),
            pltpu.SemaphoreType.DMA((9,)),
        ],
        compiler_params=pltpu.CompilerParams(
            collective_id=0, has_side_effects=True, vmem_limit_bytes=60 * 2**20
        ),
    )(features, short_filters, long_filter, cotangent, *map(jnp.asarray, (turn, waves, shift, spots, edge)))
    return pl.pallas_call(
        relay_kernel,
        out_shape=shapes,
        in_specs=[hbm] * 3,
        out_specs=(hbm,) * 3,
        scratch_shapes=[
            pltpu.VMEM((3, CH, POS), F32),
            pltpu.VMEM((3, 3, CH), F32),
            pltpu.VMEM((CH, POS), F32),
            pltpu.SemaphoreType.DMA((2, 5)),
        ],
        compiler_params=pltpu.CompilerParams(vmem_limit_bytes=60 * 2**20),
    )(*results)


def solution(mesh):
    return jax.shard_map(
        body,
        mesh=mesh,
        in_specs=(P(None, "tp", "ctx"), P(None, None, "tp"), P("tp", "ctx"), P("tp", "ctx")),
        out_specs=(P(None, "tp", "ctx"), P(None, None, "tp"), P("tp", "ctx")),
        check_vma=False,
    )
```

```python
import functools
import math

import jax
import jax.numpy as jnp
import numpy as np
from jax import lax
from jax.experimental import pallas as pl
from jax.experimental.pallas import tpu as pltpu
from jax.sharding import PartitionSpec as P

MESH = pl.DeviceIdType.MESH
F32, BF16 = jnp.float32, jnp.bfloat16
BLOCKS = 32
PLANE = 16
POS = 128
CH = 1024
OWN = CH // BLOCKS
HALF = OWN // 2
TOTAL = BLOCKS * POS
ROWS = BLOCKS * HALF


def tables():
    k = np.arange(BLOCKS)[:, None] + 0.25
    angle = 2.0 * np.pi * k * np.arange(POS)[None, :] / TOTAL
    turn = np.stack([np.cos(angle), np.sin(angle)], axis=1).astype(np.float32)
    turn = np.broadcast_to(turn[:, :, None, :], (BLOCKS, 2, 8, POS))
    angle = 2.0 * np.pi * np.arange(POS)[:, None] * np.arange(POS)[None, :] / POS
    cos, sin = np.cos(angle), np.sin(angle)
    ahead = np.block([[cos, sin], [-sin, cos]])
    back = np.block([[cos, -sin], [sin, cos]]) / TOTAL

    def split(matrix):
        high = matrix.astype(BF16)
        low = (matrix - high.astype(np.float64)).astype(BF16)
        return np.stack([high, low])

    return np.ascontiguousarray(turn), np.concatenate([split(ahead), split(back)])


def movers():
    shift = np.zeros((4, 2 * POS, 2 * POS), np.float32)
    for n in range(POS):
        if n >= 1:
            shift[:3, n - 1, n] = 1
        if n >= 2:
            shift[:3, n - 2, POS + n] = 1
        for part in (0, POS):
            if n + 1 < POS:
                shift[3, part + n + 1, n] = 1
            if n + 2 < POS:
                shift[3, part + n + 2, POS + n] = 1
    spots = np.zeros((15 * POS, POS), np.float32)
    edge = np.zeros((2 * POS, 3 * POS), np.float32)
    for r in range(9):
        spots[r * POS : r * POS + POS, r] = 1
    for b in range(3):
        shift[b, POS + 2 * b + 1, 0] = 1
        shift[b, POS + 2 * b, POS] = 1
        shift[b, POS + 2 * b + 1, POS + 1] = 1
        for part in range(2):
            for t in range(2):
                spots[(9 + 2 * b + part) * POS + t, 16 + 2 * b + t] = 1
                edge[part * POS + 2 * b + t, POS * b + 126 + t] = 1
    return shift.astype(BF16), spots.astype(BF16), edge.astype(BF16)


def add(a, b):
    return a[0] + b[0], a[1] + b[1]


def sub(a, b):
    return a[0] - b[0], a[1] - b[1]


def quarter(a, sign):
    return (-a[1], a[0]) if sign > 0 else (a[1], -a[0])


def rotate(a, angle):
    c, s = math.cos(angle), math.sin(angle)
    return a[0] * c - a[1] * s, a[0] * s + a[1] * c


def dft4(a, b, c, d, sign):
    e0, e1, o0, o1 = add(a, c), sub(a, c), add(b, d), quarter(sub(b, d), sign)
    return add(e0, o0), add(e1, o1), sub(e0, o0), sub(e1, o1)


def dft8(v, sign):
    even = dft4(v[0], v[2], v[4], v[6], sign)
    odd = dft4(v[1], v[3], v[5], v[7], sign)
    r = math.sqrt(0.5)
    a, b = odd[1], odd[3]
    if sign > 0:
        t1 = ((a[0] - a[1]) * r, (a[0] + a[1]) * r)
        t3 = ((b[0] + b[1]) * -r, (b[0] - b[1]) * r)
    else:
        t1 = ((a[0] + a[1]) * r, (a[1] - a[0]) * r)
        t3 = ((b[1] - b[0]) * r, (b[0] + b[1]) * -r)
    turned = (odd[0], t1, quarter(odd[2], sign), t3)
    return [add(e, t) for e, t in zip(even, turned)] + [sub(e, t) for e, t in zip(even, turned)]


def blocks_ahead(load, stage, turn_ref, store):
    c, s, r = math.cos(math.pi / 8), math.sin(math.pi / 8), math.sqrt(0.5)
    for b0 in range(8):
        x0, x1, x2, x3 = (load(b0 + 8 * b1) for b1 in range(4))
        x2 = x2 * r
        e0, e1 = (x0 + x2, x2), (x0 - x2, -x2)
        u1, u3 = (x1 * c, x1 * s), (x3 * s, x3 * c)
        o0, o1 = add(u1, u3), quarter(sub(u1, u3), 1)
        for k1, value in enumerate((add(e0, o0), add(e1, o1), sub(e0, o0), sub(e1, o1))):
            if b0:
                value = rotate(value, 2.0 * math.pi * (k1 + 0.25) * b0 / 32)
            stage[k1, b0, 0], stage[k1, b0, 1] = value
    for k1 in range(4):
        spectrum = dft8([(stage[k1, b0, 0], stage[k1, b0, 1]) for b0 in range(8)], 1)
        for k0, (re, im) in enumerate(spectrum):
            k = k1 + 4 * k0
            cos, sin = turn_ref[k, 0], turn_ref[k, 1]
            store(k, re * cos - im * sin, re * sin + im * cos)


def blocks_back(load, stage, turn_ref, store):
    for k1 in range(4):
        terms = []
        for k0 in range(8):
            k = k1 + 4 * k0
            re, im = load(k)
            cos, sin = turn_ref[k, 0], turn_ref[k, 1]
            terms.append((re * cos + im * sin, im * cos - re * sin))
        for b0, value in enumerate(dft8(terms, -1)):
            if b0:
                value = rotate(value, -2.0 * math.pi * (k1 + 0.25) * b0 / 32)
            stage[k1, b0, 0], stage[k1, b0, 1] = value
    for b0 in range(8):
        terms = [(stage[k1, b0, 0], stage[k1, b0, 1]) for k1 in range(4)]
        for b1, (re, im) in enumerate(dft4(*terms, -1)):
            angle = math.pi * b1 / 8
            store(b0 + 8 * b1, re * math.cos(angle) + im * math.sin(angle) if b1 else re)


def halves(values):
    high = values.astype(BF16)
    return high, (values - high.astype(F32)).astype(BF16)


def product(values, weights):
    high, low = halves(values)
    dot = functools.partial(jnp.dot, preferred_element_type=F32)
    return dot(high, weights[0]) + dot(low, weights[0]) + dot(high, weights[1])


def kernel(
    feat_hbm, taps_hbm, filt_hbm, cot_hbm, turn_hbm, waves_hbm, shift_hbm, spots_hbm, edge_hbm,
    fgrad_hbm, sgrad_hbm, lgrad_hbm,
    fgrad, sgrad, lgrad, feat, taps, filt, cot, turn, waves, shift, spots, edge,
    taps_t, rim_t, wide, shifted, mixed, pieces, dots, moved, halo_out, halo_in,
    go_out, filt_in, go_in, times, freqs, spec, paired, filt_spec, stage, conv_out, long_out, conv_in, long_in,
    sums, sums_t, part_out, part_in, whole_in, rim_out, rim_in,
    send, recv, conv_recv, local,
):
    me = lax.axis_index("ctx")
    low = lax.rem(me, PLANE)
    plane = me - low

    def to(device):
        return {"ctx": device}

    def each(count, step, unroll=1):
        lax.fori_loop(0, count, lambda i, c: (step(i), c)[1], 0, unroll=unroll)

    def remote(src, dst, sem, device):
        return pltpu.make_async_remote_copy(
            src_ref=src, dst_ref=dst, send_sem=send.at[sem], recv_sem=recv.at[sem],
            device_id=to(device), device_id_type=MESH,
        )

    def await_all(ref, sem, way):
        pltpu.make_async_copy(ref, ref, way.at[sem]).wait()

    def across(i):
        return PLANE - plane + lax.rem(low + i, PLANE)

    def within(i):
        return plane + lax.rem(low + i + 1, PLANE)

    def to_all(step):
        each(PLANE, lambda i: step(across(i)))
        each(PLANE - 1, lambda i: step(within(i)))

    loads = [
        pltpu.make_async_copy(src, dst, local.at[i])
        for i, (src, dst) in enumerate(
            (
                (feat_hbm, feat), (filt_hbm, filt), (taps_hbm, taps), (shift_hbm, shift), (cot_hbm, cot),
                (turn_hbm, turn), (waves_hbm, waves), (spots_hbm, spots), (edge_hbm, edge),
            )
        )
    ]
    barrier = pltpu.get_barrier_semaphore()
    def signal(p):
        pl.semaphore_signal(barrier, inc=1, device_id=to(p), device_id_type=MESH)

    each(PLANE - 1, lambda i: signal(within(i)))
    each(PLANE, lambda i: signal(across(i)))
    for load in loads:
        load.start()

    row = lax.broadcasted_iota(jnp.int32, (16, POS), 0)
    lane = lax.broadcasted_iota(jnp.int32, (16, POS), 1)
    rim = jnp.zeros((16, CH), F32)
    loads[0].wait()
    for b in range(3):
        pick = (lane == row + (126 - 2 * b)) & (row >= 2 * b) & (row < 2 * b + 2)
        rim = rim + lax.dot_general(
            pick.astype(BF16), feat[b], (((1,), (1,)), ((), ())), preferred_element_type=F32
        )
    halo_out[...] = rim.astype(BF16)
    loads[1].wait()
    pl.semaphore_wait(barrier, BLOCKS - 1)

    @pl.when(me < BLOCKS - 1)
    def _():
        remote(halo_out, halo_in, 0, me + 1).start()

    def send_filter(p):
        remote(filt.at[pl.ds(pl.multiple_of(p * OWN, OWN), OWN)], filt_in.at[me], 1, p).start()

    to_all(send_filter)
    filt_in[me] = filt[pl.ds(pl.multiple_of(me * OWN, OWN), OWN), :]

    for load in loads[2:]:
        load.wait()
    taps_t[...] = jnp.zeros_like(taps_t)
    for b in range(3):
        taps_t[3 * b : 3 * b + 3, :] = taps[b].astype(F32)
    turned = taps_t[...].T.astype(BF16)
    from_row = lax.broadcasted_iota(jnp.int32, (POS, POS), 0)
    for r in range(9):
        wide[r] = jnp.dot(turned, (from_row == r).astype(BF16), preferred_element_type=F32)


    rim_t[...] = jnp.zeros_like(rim_t)

    @pl.when(me > 0)
    def _():
        remote(halo_out, halo_in, 0, me).wait_recv()
        rim_t[0:16, :] = halo_in[...].astype(F32)

    behind = rim_t[...].T.astype(BF16)
    for b in range(3):
        shifted[b] = jnp.dot(
            jnp.concatenate([feat[b], behind], axis=1), shift[b], preferred_element_type=F32
        ).astype(BF16)

    def make_go(r0, target):
        rows = pl.ds(r0, 16)
        m = []
        for b in range(3):
            x = feat[b, rows, :].astype(F32)
            x1, x2 = shifted[b, rows, 0:POS].astype(F32), shifted[b, rows, POS : 2 * POS].astype(F32)
            m.append(wide[3 * b, rows, :] * x + wide[3 * b + 1, rows, :] * x1 + wide[3 * b + 2, rows, :] * x2)
        mixed[0, rows, :], mixed[1, rows, :] = m[1], m[2]
        target[0] = (m[1] * m[2]).astype(BF16)
        target[1] = (cot[rows, :].astype(F32) * m[0]).astype(BF16)

    for h in range(2):

        def send_go(p, h=h):
            make_go(pl.multiple_of(p * OWN + HALF * h, 16), go_out.at[h, p])
            remote(go_out.at[h, p], go_in.at[h, me], 2 + h, p).start()

        to_all(send_go)
        make_go(pl.multiple_of(me * OWN + HALF * h, 16), go_in.at[h, me])

    def spectra(first, count):
        def ahead(i):
            s, q = first + i // 2, pl.multiple_of(lax.rem(i, 2) * 8, 8)

            def store(k, re, im):
                freqs[s, pl.ds(k * HALF + q, 8), 0:POS] = re
                freqs[s, pl.ds(k * HALF + q, 8), POS : 2 * POS] = im

            blocks_ahead(lambda b: times[s, b, pl.ds(q, 8), :], stage, turn, store)

        each(2 * count, ahead)

    def signals(s, target):
        def back(i):
            q = pl.multiple_of(lax.rem(i, 2) * 8, 8)
            n = s + i // 2

            def load(k):
                rows = pl.ds(k * HALF + q, 8)
                return spec[n, rows, 0:POS], spec[n, rows, POS : 2 * POS]

            def store(b, value):
                times[n, b, pl.ds(q, 8), :] = value

            blocks_back(load, stage, turn, store)

        each(2 * target, back)

    def inverse(values):
        dot = functools.partial(jnp.dot, preferred_element_type=F32)
        return dot(values, waves[2]) + dot(values, waves[3])

    def transform_filter(h):
        def spread(b):
            times[0, b] = filt_in[b, HALF * h : HALF * h + HALF, :].astype(F32)

        each(BLOCKS, spread, 4)
        spectra(0, 1)
        filt_spec[h] = product(freqs[0], waves.at[0:2])

    def transform(h):
        def spread(b):
            times[1, b] = go_in[h, b, 0].astype(F32)
            times[2, b] = go_in[h, b, 1].astype(F32)

        each(BLOCKS, spread, 4)
        spectra(1, 2)
        for s in (1, 2):
            spec[s] = product(freqs[s], waves.at[0:2])

        def pairs(i):
            rows = pl.ds(pl.multiple_of(i * 16, 16), 16)
            f = filt_spec[h, rows, 0:POS], filt_spec[h, rows, POS : 2 * POS]
            g, o = ((spec[s, rows, 0:POS], spec[s, rows, POS : 2 * POS]) for s in (1, 2))
            both = (
                (f[0] * g[0] - f[1] * g[1], f[0] * g[1] + f[1] * g[0]),
                (f[0] * o[0] + f[1] * o[1], f[0] * o[1] - f[1] * o[0]),
                (g[0] * o[0] + g[1] * o[1], g[0] * o[1] - g[1] * o[0]),
            )
            for s, (re, im) in enumerate(both):
                paired[h, s, rows, 0:POS] = re.astype(BF16)
                paired[h, s, rows, POS : 2 * POS] = im.astype(BF16)

        each(ROWS // 16, pairs, 2)
        for s in range(2):
            spec[s] = inverse(paired[h, s])
        signals(0, 2)

        def pack(b):
            conv_out[h, b, 0] = times[0, b].astype(BF16)
            conv_out[h, b, 1] = times[1, b].astype(BF16)

        each(BLOCKS, pack, 4)

    def transform_long(h):
        spec[2] = inverse(paired[h, 2])
        signals(2, 1)

        def pack(b):
            long_out[h, b] = times[2, b].astype(BF16)

        each(BLOCKS, pack, 4)

    def send_conv(h):
        def step(p):
            pltpu.make_async_remote_copy(
                src_ref=conv_out.at[h, p], dst_ref=conv_in.at[h, me], send_sem=send.at[4 + h],
                recv_sem=conv_recv.at[h, me], device_id=to(p), device_id_type=MESH,
            ).start()

        to_all(step)
        conv_in[h, me] = conv_out[h, me]

    await_all(filt_in.at[0 : BLOCKS - 1], 1, recv)
    for h in range(2):
        transform_filter(h)
    await_all(go_in.at[0, 0 : BLOCKS - 1], 2, recv)
    transform(0)
    send_conv(0)
    await_all(go_in.at[1, 0 : BLOCKS - 1], 3, recv)
    transform(1)
    send_conv(1)
    for h in range(2):
        transform_long(h)
    def finish(h, e):
        rows = pl.ds(pl.multiple_of(e * OWN + HALF * h, 16), 16)
        here = pl.ds(pl.multiple_of(e * HALF, 16), 16)
        conv, grad = conv_in[h, e, 0].astype(F32), conv_in[h, e, 1].astype(F32)
        branch = (cot[rows, :].astype(F32) * conv, grad * mixed[1, rows, :], grad * mixed[0, rows, :])
        for b, g in enumerate(branch):
            pieces[h, b, here, 0:POS], pieces[h, b, here, POS : 2 * POS] = halves(g)
            past = (
                feat[b, rows, :], shifted[b, rows, 0:POS], shifted[b, rows, POS : 2 * POS]
            )
            for j, x in enumerate(past):
                k = (3 * b + j) * POS
                dots[here, k : k + POS] = (g * x.astype(F32)).astype(BF16)

    def add_up(h):
        dot = functools.partial(jnp.dot, preferred_element_type=F32)
        sums[:, h] = dot(dots[...], spots[0 : 9 * POS, :]).reshape(BLOCKS, HALF, POS)

    def add_rims():
        dot = functools.partial(jnp.dot, preferred_element_type=F32)
        for h in range(2):
            total = jnp.zeros((ROWS, POS), F32)
            for b in range(3):
                k = (9 + 2 * b) * POS
                total = total + dot(pieces[h, b], spots[k : k + 2 * POS, :])
            sums[:, h] = total.reshape(BLOCKS, HALF, POS)
        rim_t[...] = sums[...].reshape(CH, POS).T

    def trail(h):
        for b in range(3):
            moved[b] = jnp.dot(pieces[h, b], shift[3], preferred_element_type=F32)

        def step(e):
            rows = pl.ds(pl.multiple_of(e * OWN + HALF * h, 16), 16)
            here = pl.ds(pl.multiple_of(e * HALF, 16), 16)
            for b in range(3):
                g = pieces[h, b, here, 0:POS].astype(F32) + pieces[h, b, here, POS : 2 * POS].astype(F32)
                fgrad[b, rows, :] = (
                    wide[3 * b, rows, :] * g
                    + wide[3 * b + 1, rows, :] * moved[b, here, 0:POS]
                    + wide[3 * b + 2, rows, :] * moved[b, here, POS : 2 * POS]
                )

        each(BLOCKS, step, 2)

    for h in range(2):
        finish(h, me)

        def arrived(e, h=h):
            pltpu.make_async_copy(conv_in.at[h, e], conv_in.at[h, e], conv_recv.at[h, e]).wait()
            finish(h, e)

        each(PLANE - 1, lambda i: arrived(plane + lax.rem(low + PLANE - 1 - i, PLANE)))
        each(PLANE, lambda i: arrived(PLANE - plane + lax.rem(low + PLANE - i, PLANE)))
        add_up(h)
        if h == 0:
            trail(h)

        if h == 0:
            await_all(conv_out.at[1, 0 : BLOCKS - 1], 5, send)
            for k in range(2):

                def send_long(p, k=k):
                    remote(long_out.at[k, p], long_in.at[k, me], 6 + k, p).start()

                to_all(send_long)
                long_in[k, me] = long_out[k, me]


    sums_t[...] = sums[...].reshape(CH, POS).T

    for r in range(9):
        for c in range(8):
            q, k = (8 * r + c) // 5, (8 * r + c) % 5
            part_out[q, k : k + 1] = sums_t[r : r + 1, POS * c : POS * c + POS]

    part_out[14, 2:5] = jnp.zeros((3, POS), F32)
    part_out[15] = jnp.zeros((5, POS), F32)

    def send_part(i):
        q = lax.rem(low + i + 1, PLANE)
        remote(part_out.at[q], part_in.at[low], 9, plane + q).start()

    each(PLANE - 1, send_part)
    part_in[low] = part_out[low]

    add_rims()
    rim_out[...] = rim_t[16:24, :]

    @pl.when(me > 0)
    def _():
        remote(rim_out, rim_in, 8, me - 1).start()

    trail(1)
    await_all(part_in.at[0 : PLANE - 1], 9, recv)
    total = part_in[0]
    for q in range(1, PLANE):
        total = total + part_in[q]
    whole_in[me] = total

    to_all(lambda p: remote(whole_in.at[me], whole_in.at[me], 10, p).start())

    stores = [
        pltpu.make_async_copy(src, dst, local.at[i])
        for i, (src, dst) in enumerate(((fgrad, fgrad_hbm), (sgrad, sgrad_hbm), (lgrad, lgrad_hbm)))
    ]
    rim_t[...] = jnp.zeros_like(rim_t)

    @pl.when(me < BLOCKS - 1)
    def _():
        remote(rim_in, rim_in, 8, me).wait_recv()
        for b in range(3):
            first, second = rim_in[2 * b : 2 * b + 1, :], rim_in[2 * b + 1 : 2 * b + 2, :]
            w1, w2 = taps_t[3 * b + 1 : 3 * b + 2, :], taps_t[3 * b + 2 : 3 * b + 3, :]
            rim_t[2 * b : 2 * b + 1, :] = w2 * first
            rim_t[2 * b + 1 : 2 * b + 2, :] = w1 * first + w2 * second

    beyond = jnp.dot(
        jnp.concatenate(halves(rim_t[...].T), axis=1), edge[...], preferred_element_type=F32
    )
    for b in range(3):
        fgrad[b] += beyond[:, POS * b : POS * b + POS]
    stores[0].start()

    for h in range(2):
        await_all(long_in.at[h, 0 : BLOCKS - 1], 6 + h, recv)

        def unpack(e, h=h):
            rows = pl.ds(pl.multiple_of(e * OWN + HALF * h, 16), 16)
            lgrad[rows, :] = long_in[h, e].astype(F32)

        each(BLOCKS, unpack)

    stores[2].start()

    await_all(whole_in.at[0 : BLOCKS - 1], 10, recv)
    for r in range(9):
        for c in range(8):
            q, k = (8 * r + c) // 5, (8 * r + c) % 5
            sgrad[r // 3, r % 3 : r % 3 + 1, POS * c : POS * c + POS] = (
                whole_in[q, k : k + 1] + whole_in[PLANE + q, k : k + 1]
            )
    stores[1].start()

    @pl.when(me < BLOCKS - 1)
    def _():
        remote(halo_out, halo_in, 0, me).wait_send()

    @pl.when(me > 0)
    def _():
        remote(rim_out, rim_in, 8, me).wait_send()

    await_all(filt_in.at[0 : BLOCKS - 1], 1, send)
    for h in range(2):
        await_all(go_out.at[h, 0 : BLOCKS - 1], 2 + h, send)
        if h == 0:
            await_all(conv_out.at[h, 0 : BLOCKS - 1], 4 + h, send)
        await_all(long_out.at[h, 0 : BLOCKS - 1], 6 + h, send)
    await_all(part_out.at[0 : PLANE - 1], 9, send)
    await_all(whole_in.at[0 : BLOCKS - 1], 10, send)
    for store in stores:
        store.wait()


def relay_kernel(fgrad, sgrad, lgrad, fgrad_out, sgrad_out, lgrad_out, fgrad_v, sgrad_v, lgrad_v, sems):
    parts = [(fgrad.at[b], fgrad_v.at[b], fgrad_out.at[b]) for b in range(3)]
    parts += [(lgrad, lgrad_v, lgrad_out), (sgrad, sgrad_v, sgrad_out)]
    loads = [pltpu.make_async_copy(a, b, sems.at[0, i]) for i, (a, b, _) in enumerate(parts)]
    stores = [pltpu.make_async_copy(b, c, sems.at[1, i]) for i, (_, b, c) in enumerate(parts)]
    for load in loads:
        load.start()
    for load, store in zip(loads, stores):
        load.wait()
        store.start()
    for store in stores:
        store.wait()


def body(features, short_filters, long_filter, cotangent):
    turn, waves = tables()
    shift, spots, edge = movers()
    hbm = pl.BlockSpec(memory_space=pl.ANY)
    shapes = (
        jax.ShapeDtypeStruct((3, CH, POS), F32),
        jax.ShapeDtypeStruct((3, 3, CH), F32),
        jax.ShapeDtypeStruct((CH, POS), F32),
    )
    results = pl.pallas_call(
        kernel,
        out_shape=shapes,
        in_specs=[hbm] * 9,
        out_specs=(hbm,) * 3,
        scratch_shapes=[
            pltpu.VMEM((3, CH, POS), F32),
            pltpu.VMEM((3, 3, CH), F32),
            pltpu.VMEM((CH, POS), F32),
            pltpu.VMEM((3, CH, POS), BF16),
            pltpu.VMEM((3, 3, CH), BF16),
            pltpu.VMEM((CH, POS), BF16),
            pltpu.VMEM((CH, POS), BF16),
            pltpu.VMEM((BLOCKS, 2, 8, POS), F32),
            pltpu.VMEM((4, 2 * POS, 2 * POS), BF16),
            pltpu.VMEM((4, 2 * POS, 2 * POS), BF16),
            pltpu.VMEM((15 * POS, POS), BF16),
            pltpu.VMEM((2 * POS, 3 * POS), BF16),
            pltpu.VMEM((POS, CH), F32),
            pltpu.VMEM((POS, CH), F32),
            pltpu.VMEM((9, CH, POS), F32),
            pltpu.VMEM((3, CH, 2 * POS), BF16),
            pltpu.VMEM((2, CH, POS), F32),
            pltpu.VMEM((2, 3, ROWS, 2 * POS), BF16),
            pltpu.VMEM((ROWS, 9 * POS), BF16),
            pltpu.VMEM((3, ROWS, 2 * POS), F32),
            pltpu.VMEM((16, CH), BF16),
            pltpu.VMEM((16, CH), BF16),
            pltpu.VMEM((2, BLOCKS, 2, HALF, POS), BF16),
            pltpu.VMEM((BLOCKS, OWN, POS), BF16),
            pltpu.VMEM((2, BLOCKS, 2, HALF, POS), BF16),
            pltpu.VMEM((3, BLOCKS, HALF, POS), F32),
            pltpu.VMEM((3, ROWS, 2 * POS), F32),
            pltpu.VMEM((3, ROWS, 2 * POS), F32),
            pltpu.VMEM((2, 3, ROWS, 2 * POS), BF16),
            pltpu.VMEM((2, ROWS, 2 * POS), F32),
            pltpu.VMEM((4, 8, 2, 8, POS), F32),
            pltpu.VMEM((2, BLOCKS, 2, HALF, POS), BF16),
            pltpu.VMEM((2, BLOCKS, HALF, POS), BF16),
            pltpu.VMEM((2, BLOCKS, 2, HALF, POS), BF16),
            pltpu.VMEM((2, BLOCKS, HALF, POS), BF16),
            pltpu.VMEM((BLOCKS, 2, HALF, POS), F32),
            pltpu.VMEM((POS, CH), F32),
            pltpu.VMEM((PLANE, 5, POS), F32),
            pltpu.VMEM((PLANE, 5, POS), F32),
            pltpu.VMEM((BLOCKS, 5, POS), F32),
            pltpu.VMEM((8, CH), F32),
            pltpu.VMEM((8, CH), F32),
            pltpu.SemaphoreType.DMA((11,)),
            pltpu.SemaphoreType.DMA((11,)),
            pltpu.SemaphoreType.DMA((2, BLOCKS)),
            pltpu.SemaphoreType.DMA((9,)),
        ],
        compiler_params=pltpu.CompilerParams(
            collective_id=0, has_side_effects=True, vmem_limit_bytes=60 * 2**20
        ),
    )(features, short_filters, long_filter, cotangent, *map(jnp.asarray, (turn, waves, shift, spots, edge)))
    return pl.pallas_call(
        relay_kernel,
        out_shape=shapes,
        in_specs=[hbm] * 3,
        out_specs=(hbm,) * 3,
        scratch_shapes=[
            pltpu.VMEM((3, CH, POS), F32),
            pltpu.VMEM((3, 3, CH), F32),
            pltpu.VMEM((CH, POS), F32),
            pltpu.SemaphoreType.DMA((2, 5)),
        ],
        compiler_params=pltpu.CompilerParams(vmem_limit_bytes=60 * 2**20),
    )(*results)


def solution(mesh):
    return jax.shard_map(
        body,
        mesh=mesh,
        in_specs=(P(None, "tp", "ctx"), P(None, None, "tp"), P("tp", "ctx"), P("tp", "ctx")),
        out_specs=(P(None, "tp", "ctx"), P(None, None, "tp"), P("tp", "ctx")),
        check_vma=False,
    )
```
